256 devices in a mesh: wa: 32 (over x, z), gz: 8 (over y, core).
Axes of the slice: x: 4, y: 4, z: 8, core: 2. Of those that a mesh axis runs over, the one named last changes fastest.
Arguments:
- tensor: float32 [4, 64, 1024, 1024], P(None, 'gz', 'wa')
- start: float32 [1024, 128], replicated, may hold values from -6 to 6
Outputs:
- factor: float32 [1024, 128], replicated
- core: float32 [4, 64, 128, 1024], P(None, 'gz', None, 'wa')
The draws below stay inside these ranges and needn't reach their ends.
All inputs are finite; a program needn't handle non-finite values.
Results may differ from the reference program's by a relative error of at most 0.00018.
Values sent between devices are 32-bit elements; how exact they have to be, the bound alone decides.
A program may use at most 128 MiB of HBM per device.

```python
import jax
import jax.numpy as jnp
from jax import lax

NX = 1024
NY = 1024
RANK = 128
S = 4
ITERS = 4
NZ = 64


def draw_tensor(key, part):
    key = jax.random.fold_in(key, 11)
    key_scale, key_base = jax.random.split(key, 2)
    log_scale = jax.random.uniform(key_scale, (1, 1, NX, 1), jnp.float32, 0.0, 1.0986)
    base = jax.random.normal(key_base, (S, NZ, NX, NY), jnp.float32)
    return (base * jnp.exp(log_scale)).astype(jnp.float32)


def scatter_about(key, dims, width, limit, dtype=jnp.bfloat16):
    entries = width * jax.random.normal(key, dims, jnp.float32)
    return jnp.clip(entries, min=-limit, max=limit).astype(dtype)


def setup_inputs(seed: int = 0) -> dict:
    key_of = jax.random.split(jax.random.key(seed), 3)
    tensor = draw_tensor(jax.random.fold_in(key_of[2], 71), 0)
    start = scatter_about(key_of[1], (NX, RANK), 1.0, 6.0, jnp.float32)
    return {"tensor": tensor, "start": start}


def reference(tensor, start):
    scale_total = 1.0 / (NY * NZ * S)

    def add_sample(total, block):
        term = jnp.einsum('zay,zby->ab', block, block, precision=lax.Precision.HIGHEST)
        return (total + term, None)
    gram, unused = lax.scan(add_sample, jnp.zeros((NX, NX), jnp.float32), tensor)
    gram = gram * scale_total
    basis = start
    for step in range(ITERS):
        image = jnp.dot(gram, basis, precision=lax.Precision.HIGHEST)
        small = jnp.dot(image.T, image, precision=lax.Precision.HIGHEST)
        lower = jnp.linalg.cholesky(small)
        basis = lax.linalg.triangular_solve(lower, image, left_side=False, lower=True, transpose_a=True)
    core = jnp.einsum('ar,szay->szry', basis, tensor, precision=lax.Precision.HIGHEST)
    return (basis, core)
```

```python
import functools

import jax
import jax.numpy as jnp
from jax import lax
from jax.experimental import pallas as pl
from jax.experimental.pallas import tpu as pltpu
from jax.sharding import PartitionSpec as P

MESH = pl.DeviceIdType.MESH
ITERS = 4
NX = 1024
RANK = 128
KX, KY, KZ = 4, 4, 8
NWA = KX * KZ
PLANES = 32
CHUNKS = 4
PAIRS = [(0, 0), (0, 1), (1, 1), (0, 2), (1, 2), (2, 2), (0, 3), (1, 3), (2, 3), (3, 3)]
BLOCKS = 12
SLOT = [0, 1, 2, 4, 5, 6, 8, 9, 10, 11]
F32, BF16 = jnp.float32, jnp.bfloat16
NT = (((1,), (1,)), ((), ()))


def split(values):
    high = values.astype(BF16)
    return high, (values - high.astype(F32)).astype(BF16)


def pack_tile(loaded, packed, chunk, quad):
    lane = lax.broadcasted_iota(jnp.int32, (8, 128), 1)
    low_half = lane < 64
    even_quarter = lax.rem(lane, 64) < 32
    for group in range(8):
        columns = pl.ds(128 * group, 128)
        v = [loaded[chunk, 4 * quad + m, :, columns] for m in range(4)]
        a = [None] * 4
        for m in range(2):
            a[m] = jnp.where(low_half, v[m], pltpu.roll(v[m + 2], 64, 1))
            a[m + 2] = jnp.where(low_half, pltpu.roll(v[m], 64, 1), v[m + 2])
        out = []
        for m in (0, 2):
            out.append(jnp.where(even_quarter, a[m], pltpu.roll(a[m + 1], 32, 1)))
            out.append(jnp.where(even_quarter, pltpu.roll(a[m], 96, 1), a[m + 1]))
        for m in range(4):
            packed[chunk, 4 * group + m, :, pl.ds(pl.multiple_of(128 * quad, 128), 128)] = out[m]


def regroup_kernel(tensor, high, low, gram, loaded, packed, landed, load_sem, send_sem, recv_sem):
    me = lax.axis_index("wa")

    def peer(step):
        return lax.rem(me + step, NWA)

    def load(chunk):
        return pltpu.make_async_copy(
            tensor.at[:, pl.ds(8 * chunk, 8), :], loaded.at[chunk], load_sem.at[chunk]
        )

    for chunk in range(CHUNKS):
        load(chunk).start()
    barrier = pltpu.get_barrier_semaphore()

    @pl.loop(1, NWA)
    def _(step):
        pl.semaphore_signal(barrier, inc=1, device_id={"wa": peer(step)}, device_id_type=MESH)

    pl.semaphore_wait(barrier, NWA - 1)

    for chunk in range(CHUNKS):
        load(chunk).wait()

        @pl.loop(0, PLANES // 4)
        def _(quad):
            pack_tile(loaded, packed, chunk, quad)

        @pl.loop(1, NWA)
        def _(step):
            to = peer(step)
            pltpu.make_async_remote_copy(
                src_ref=packed.at[chunk, to],
                dst_ref=landed.at[chunk, me],
                send_sem=send_sem.at[chunk],
                recv_sem=recv_sem.at[chunk],
                device_id={"wa": to},
                device_id_type=MESH,
            ).start()

        landed[chunk, me] = packed[chunk, me]

    for chunk in range(CHUNKS):
        others = landed.at[chunk, pl.ds(0, NWA - 1)]
        pltpu.make_async_copy(others, others, recv_sem.at[chunk]).wait()
        rows = pl.ds(256 * chunk, 256)
        high[rows, :], low[rows, :] = split(landed[chunk].reshape(256, NX))
        for slot, (b, c) in zip(SLOT, PAIRS):
            if c != chunk:
                continue
            hb, lb = high[pl.ds(256 * b, 256), :], low[pl.ds(256 * b, 256), :]
            hc, lc = high[rows, :], low[rows, :]
            dot = functools.partial(lax.dot_general, dimension_numbers=NT, preferred_element_type=F32)
            block = dot(hb, hc) + (dot(hb, lc) + dot(lb, hc))
            gram[slot, 0] = block[:, :128]
            gram[slot, 1] = block[:, 128:]
    for slot in (3, 7):
        gram[slot] = jnp.zeros((2, 256, 128), F32)
    for chunk in range(CHUNKS):
        others = packed.at[chunk, pl.ds(0, NWA - 1)]
        pltpu.make_async_copy(others, others, send_sem.at[chunk]).wait()


def regroup(tensor):
    return pl.pallas_call(
        regroup_kernel,
        out_shape=(
            jax.ShapeDtypeStruct((NX, NX), BF16),
            jax.ShapeDtypeStruct((NX, NX), BF16),
            jax.ShapeDtypeStruct((BLOCKS, 2, 256, 128), F32),
        ),
        in_specs=[pl.BlockSpec(memory_space=pl.ANY)],
        out_specs=(pl.BlockSpec(memory_space=pltpu.VMEM),) * 3,
        scratch_shapes=[
            pltpu.VMEM((CHUNKS, PLANES, 8, NX), F32),
            pltpu.VMEM((CHUNKS, NWA, 8, NX), F32),
            pltpu.VMEM((CHUNKS, NWA, 8, NX), F32),
            pltpu.SemaphoreType.DMA((CHUNKS,)),
            pltpu.SemaphoreType.DMA((CHUNKS,)),
            pltpu.SemaphoreType.DMA((CHUNKS,)),
        ],
        compiler_params=pltpu.CompilerParams(
            collective_id=0, has_side_effects=True, vmem_limit_bytes=48 * 1024 * 1024
        ),
        name="regroup_gram",
    )(tensor)


def reduce_kernel(gram, out, from_core, mine, from_xy, sums, from_z, final, gathered, part, sem):
    wa, gz = lax.axis_index("wa"), lax.axis_index("gz")
    x, z = wa // KZ, lax.rem(wa, KZ)
    y, core = gz // 2, lax.rem(gz, 2)
    me_xy = x * KY + y
    other = 1 - core

    def xy_peer(step):
        q = lax.rem(me_xy + step, KX * KY)
        return q, {"wa": (q // KY) * KZ + z, "gz": lax.rem(q, KY) * 2 + core}

    def z_peer(step):
        q = lax.rem(z + step, KZ)
        return q, {"wa": x * KZ + q}

    def send(src, dst, k, device):
        pltpu.make_async_remote_copy(
            src_ref=src, dst_ref=dst, send_sem=sem.at[0, k], recv_sem=sem.at[1, k],
            device_id=device, device_id_type=MESH,
        ).start()

    def wait(ref, k):
        pltpu.make_async_copy(ref, ref, sem.at[1, k]).wait()

    def wait_sent(ref, k):
        pltpu.make_async_copy(ref, ref, sem.at[0, k]).wait()

    barrier = pltpu.get_barrier_semaphore()
    pl.semaphore_signal(barrier, inc=1, device_id={"gz": y * 2 + other}, device_id_type=MESH)

    @pl.loop(1, KX * KY)
    def _(step):
        pl.semaphore_signal(barrier, inc=1, device_id=xy_peer(step)[1], device_id_type=MESH)

    @pl.loop(1, KZ)
    def _(step):
        pl.semaphore_signal(barrier, inc=1, device_id=z_peer(step)[1], device_id_type=MESH)

    pl.semaphore_wait(barrier, 1 + KX * KY - 1 + KZ - 1)

    send(gram.at[:, other], from_core, 0, {"gz": y * 2 + other})
    wait(from_core, 0)
    for b in range(BLOCKS):
        both = gram[b, core] + from_core[b]
        mine[:, b] = both.reshape(16, 16, 128)

    @pl.loop(1, KX * KY)
    def _(step):
        q, device = xy_peer(step)
        send(mine.at[q], from_xy.at[me_xy], 1, device)

    from_xy[me_xy] = mine[me_xy]
    wait(from_xy.at[pl.ds(0, 15)], 1)
    total = from_xy[0]
    for q in range(1, 16):
        total = total + from_xy[q]
    sums[...] = total.reshape(KZ, BLOCKS * 2, 128)

    @pl.loop(1, KZ)
    def _(step):
        q, device = z_peer(step)
        send(sums.at[q], from_z.at[z], 2, device)

    from_z[z] = sums[z]
    wait(from_z.at[pl.ds(0, KZ - 1)], 2)
    total = from_z[0]
    for q in range(1, KZ):
        total = total + from_z[q]
    final[...] = total
    gathered[z] = total

    @pl.loop(1, KZ)
    def _(step):
        q, device = z_peer(step)
        send(final, gathered.at[z], 3, device)

    wait(gathered.at[pl.ds(0, KZ - 1)], 3)
    rows = pl.ds(pl.multiple_of(16 * me_xy, 16), 16)
    part[...] = gathered[...].reshape(BLOCKS, 16, 128)

    @pl.loop(1, KX * KY)
    def _(step):
        q, device = xy_peer(step)
        send(part, out.at[:, core, rows, :], 4, device)

    out[:, core, rows, :] = part[...]
    wait(out.at[:, 0, pl.ds(0, 240), :], 4)
    send(out.at[:, core], out.at[:, core], 5, {"gz": y * 2 + other})
    wait(out.at[:, other], 5)
    wait_sent(from_core, 0)
    wait_sent(mine.at[pl.ds(0, 15)], 1)
    wait_sent(sums.at[pl.ds(0, KZ - 1)], 2)
    wait_sent(gathered.at[pl.ds(0, KZ - 1)], 3)
    wait_sent(mine.at[pl.ds(0, 15)], 4)
    wait_sent(from_core, 5)


def reduce_gram(gram):
    part = BLOCKS * 2
    return pl.pallas_call(
        reduce_kernel,
        out_shape=jax.ShapeDtypeStruct((BLOCKS, 2, 256, 128), F32),
        in_specs=[pl.BlockSpec(memory_space=pltpu.VMEM)],
        out_specs=pl.BlockSpec(memory_space=pltpu.VMEM),
        scratch_shapes=[
            pltpu.VMEM((BLOCKS, 256, 128), F32),
            pltpu.VMEM((16, BLOCKS, 16, 128), F32),
            pltpu.VMEM((16, BLOCKS, 16, 128), F32),
            pltpu.VMEM((KZ, part, 128), F32),
            pltpu.VMEM((KZ, part, 128), F32),
            pltpu.VMEM((part, 128), F32),
            pltpu.VMEM((KZ, part, 128), F32),
            pltpu.VMEM((BLOCKS, 16, 128), F32),
            pltpu.SemaphoreType.DMA((2, 6)),
        ],
        compiler_params=pltpu.CompilerParams(
            collective_id=1, has_side_effects=True, vmem_limit_bytes=40 * 1024 * 1024
        ),
        name="reduce_gram",
    )(gram)


def inverse_factor(small, lower_inv):
    lane = lax.broadcasted_iota(jnp.int32, (8, RANK), 1)
    row_in_tile = lax.broadcasted_iota(jnp.int32, (8, RANK), 0)
    tiles = [small[8 * t : 8 * t + 8, :] for t in range(RANK // 8)]
    for j in range(RANK):
        t, s = divmod(j, 8)
        spread = {u: jnp.broadcast_to(tiles[u][:, j : j + 1], (8, RANK)) for u in range(t, RANK // 8)}
        pivot = jnp.broadcast_to(spread[t][s : s + 1, :], (8, RANK))
        row = jnp.broadcast_to(tiles[t][s : s + 1, :], (8, RANK))
        row = jnp.where(lane == j, 1.0, row)
        scaled = row * (1.0 / pivot)
        root = lax.rsqrt(pivot)
        lower_inv[j : j + 1, :] = jnp.where(lane <= j, row * root, 0.0)[0:1, :]
        for u in range(t, RANK // 8):
            kept = jnp.where(lane == j, 0.0, tiles[u])
            changed = kept - spread[u] * scaled
            tiles[u] = jnp.where(row_in_tile > s, changed, tiles[u]) if u == t else changed
    return None


def factor_kernel(gram, start, high, low, factor, core, gram_high, gram_low, basis_ref, image_ref, lower_inv):
    scale = 1.0 / 262144
    for slot, (b, c) in zip(SLOT, PAIRS):
        block = jnp.concatenate([gram[slot, 0], gram[slot, 1]], axis=1) * scale
        rb, rc = pl.ds(256 * b, 256), pl.ds(256 * c, 256)
        if b == c:
            gram_high[rb, rc], gram_low[rb, rc] = split(block)
        else:
            gram_high[rb, rc], gram_low[rb, rc] = split(block)
            gram_high[rc, rb], gram_low[rc, rb] = split(block.T)
    for c in range(CHUNKS):
        basis_ref[pl.ds(256 * c, 256), :] = start[:, c].reshape(256, RANK)

    @pl.loop(0, ITERS)
    def _(step):
        bh, bl = split(basis_ref[...])
        both = jnp.concatenate([bh, bl], axis=1)
        for c in range(CHUNKS):
            rows = pl.ds(256 * c, 256)
            wide = jnp.dot(gram_high[rows, :], both, preferred_element_type=F32)
            cross = jnp.dot(gram_low[rows, :], bh, preferred_element_type=F32)
            image_ref[rows, :] = wide[:, :RANK] + (wide[:, RANK:] + cross)
        image = image_ref[...]
        small = lax.dot_general(
            image, image, (((0,), (0,)), ((), ())), precision=lax.Precision.HIGHEST, preferred_element_type=F32
        )
        inverse_factor(small, lower_inv)
        basis_ref[...] = lax.dot_general(
            image, lower_inv[...], NT, precision=lax.Precision.HIGHEST, preferred_element_type=F32
        )

    basis = basis_ref[...]
    for c in range(CHUNKS):
        factor[:, c] = basis[256 * c : 256 * c + 256].reshape(NWA, 8, RANK)
    fh, fl = split(basis.T)
    both = jnp.concatenate([fh, fl], axis=0)
    for q in range(8):
        columns = pl.ds(128 * q, 128)
        wide = jnp.dot(both, high[:, columns], preferred_element_type=F32)
        cross = jnp.dot(fh, low[:, columns], preferred_element_type=F32)
        tile = wide[:RANK] + (wide[RANK:] + cross)
        for m in range(4):
            core[4 * q + m] = tile[:, 32 * m : 32 * m + 32]


def factor_and_core(gram, start, high, low):
    return pl.pallas_call(
        factor_kernel,
        out_shape=(
            jax.ShapeDtypeStruct((NWA, CHUNKS, 8, RANK), F32),
            jax.ShapeDtypeStruct((PLANES, RANK, 32), F32),
        ),
        in_specs=[pl.BlockSpec(memory_space=pltpu.VMEM)] * 4,
        out_specs=(pl.BlockSpec(memory_space=pltpu.VMEM),) * 2,
        scratch_shapes=[
            pltpu.VMEM((NX, NX), BF16),
            pltpu.VMEM((NX, NX), BF16),
            pltpu.VMEM((NX, RANK), F32),
            pltpu.VMEM((NX, RANK), F32),
            pltpu.VMEM((RANK, RANK), F32),
        ],
        compiler_params=pltpu.CompilerParams(vmem_limit_bytes=48 * 1024 * 1024),
        name="factor_core",
    )(gram, start, high, low)


def per_device(tensor, start):
    high, low, gram = regroup(tensor.reshape(PLANES, 32, NX))
    gram = reduce_gram(gram)
    factor, core = factor_and_core(gram, start.reshape(NWA, CHUNKS, 8, RANK), high, low)
    return factor.reshape(NX, RANK), core.reshape(4, 8, RANK, 32)


def solution(mesh):
    placed = (P(None, "gz", "wa", None), P())
    return jax.shard_map(
        per_device,
        mesh=mesh,
        in_specs=placed,
        out_specs=(P(), P(None, "gz", None, "wa")),
        check_vma=False,
    )
```

```python
import functools

import jax
import jax.numpy as jnp
from jax import lax
from jax.experimental import pallas as pl
from jax.experimental.pallas import tpu as pltpu
from jax.sharding import PartitionSpec as P

MESH = pl.DeviceIdType.MESH
ITERS = 4
NX = 1024
RANK = 128
KX, KY, KZ = 4, 4, 8
NWA = KX * KZ
PLANES = 32
CHUNKS = 4
ROUNDS = [
    [(0, 0), (0, 1), (1, 1)],
    [(0, 2), (1, 2), (2, 2)],
    [(0, 3), (1, 3), (2, 3), (3, 3)],
]
SLOTS = 4
NXY = KX * KY
TILES = SLOTS * 2
F32, BF16 = jnp.float32, jnp.bfloat16
NT = (((1,), (1,)), ((), ()))


def split(values):
    high = values.astype(BF16)
    return high, (values - high.astype(F32)).astype(BF16)


def pack_tile(loaded, packed, chunk, quad):
    lane = lax.broadcasted_iota(jnp.int32, (8, 128), 1)
    low_half = lane < 64
    even_quarter = lax.rem(lane, 64) < 32
    for group in range(8):
        columns = pl.ds(128 * group, 128)
        v = [loaded[chunk, 4 * quad + m, :, columns] for m in range(4)]
        a = [None] * 4
        for m in range(2):
            a[m] = jnp.where(low_half, v[m], pltpu.roll(v[m + 2], 64, 1))
            a[m + 2] = jnp.where(low_half, pltpu.roll(v[m], 64, 1), v[m + 2])
        out = []
        for m in (0, 2):
            out.append(jnp.where(even_quarter, a[m], pltpu.roll(a[m + 1], 32, 1)))
            out.append(jnp.where(even_quarter, pltpu.roll(a[m], 96, 1), a[m + 1]))
        for m in range(4):
            packed[chunk, 4 * group + m, :, pl.ds(pl.multiple_of(128 * quad, 128), 128)] = out[m]


def inverse_factor(small, lower_inv):
    lane = lax.broadcasted_iota(jnp.int32, (8, RANK), 1)
    full = (8, RANK)
    count = RANK // 8
    tiles = [small[8 * t : 8 * t + 8, :] for t in range(count)]

    def columns(u, t):
        return [jnp.broadcast_to(tiles[u][:, 8 * t + s : 8 * t + s + 1], full) for s in range(8)]

    def spread(t):
        cols = columns(t, t)
        entry = {(i, s): jnp.broadcast_to(cols[s][i : i + 1, :], full) for s in range(8) for i in range(s, 8)}
        rows = []
        for s in range(8):
            row = jnp.broadcast_to(tiles[t][s : s + 1, :], full)
            inside = (lane >= 8 * t) & (lane < 8 * t + 8)
            rows.append(jnp.where(inside, jnp.where(lane == 8 * t + s, 1.0, 0.0), row))
        return entry, rows

    def update(u, t, lower, root, rows):
        cols = columns(u, t)
        inside = (lane >= 8 * t) & (lane < 8 * t + 8)
        tile = jnp.where(inside, 0.0, tiles[u])
        for k in range(8):
            cols[k] = cols[k] * root[k]
            for i in range(k + 1, 8):
                cols[i] = cols[i] - lower[i, k] * cols[k]
            tile = tile - cols[k] * rows[k]
        tiles[u] = tile

    entry, rows = spread(0)
    for t in range(count):
        root, lower = [], {}
        for k in range(8):
            root.append(lax.rsqrt(entry[k, k]))
            for i in range(k + 1, 8):
                lower[i, k] = entry[i, k] * root[k]
            for i in range(k + 1, 8):
                for j in range(k + 1, i + 1):
                    entry[i, j] = entry[i, j] - lower[i, k] * lower[j, k]
            rows[k] = rows[k] * root[k]
            for i in range(k + 1, 8):
                rows[i] = rows[i] - lower[i, k] * rows[k]
        done = rows
        if t + 1 < count:
            update(t + 1, t, lower, root, done)
            entry, rows = spread(t + 1)
        for u in range(t + 2, count):
            update(u, t, lower, root, done)
        for k in range(8):
            j = 8 * t + k
            lower_inv[j : j + 1, :] = jnp.where(lane <= j, done[k], 0.0)[0:1, :]


def kernel(
    tensor, start, factor, core_out,
    loaded, packed, landed, high, low,
    gram, from_core, mine, from_xy, sums, from_z, final, gathered, part, whole,
    gram_high, gram_low, basis_ref, image_ref, lower_inv,
    load_sem, send_sem, recv_sem, sem,
):
    me, gz = lax.axis_index("wa"), lax.axis_index("gz")
    x, z = me // KZ, lax.rem(me, KZ)
    y, core = gz // 2, lax.rem(gz, 2)
    me_xy = x * KY + y
    other = 1 - core
    sibling = {"gz": y * 2 + other}

    def peer(step):
        return lax.rem(me + step, NWA)

    def xy_peer(step):
        q = lax.rem(me_xy + step, NXY)
        return q, {"wa": (q // KY) * KZ + z, "gz": lax.rem(q, KY) * 2 + core}

    def z_peer(step):
        q = lax.rem(z + step, KZ)
        return q, {"wa": x * KZ + q}

    def load(chunk):
        return pltpu.make_async_copy(
            tensor.at[:, pl.ds(8 * chunk, 8), :], loaded.at[chunk], load_sem.at[chunk]
        )

    for chunk in range(CHUNKS):
        load(chunk).start()
    barrier = pltpu.get_barrier_semaphore()

    def greet(device):
        pl.semaphore_signal(barrier, inc=1, device_id=device, device_id_type=MESH)

    @pl.loop(1, NWA)
    def _(step):
        greet({"wa": peer(step)})

    @pl.loop(1, NXY)
    def _(step):
        greet(xy_peer(step)[1])

    greet(sibling)
    pl.semaphore_wait(barrier, NWA - 1 + NXY - 1 + 1)

    def pack(chunk):
        load(chunk).wait()

        @pl.loop(0, PLANES // 4)
        def _(quad):
            pack_tile(loaded, packed, chunk, quad)

    def send_chunk(chunk):
        @pl.loop(1, NWA)
        def _(step):
            to = peer(step)
            pltpu.make_async_remote_copy(
                src_ref=packed.at[chunk, to],
                dst_ref=landed.at[chunk, me],
                send_sem=send_sem.at[chunk],
                recv_sem=recv_sem.at[chunk],
                device_id={"wa": to},
                device_id_type=MESH,
            ).start()

        landed[chunk, me] = packed[chunk, me]

    def take_chunk(chunk):
        others = landed.at[chunk, pl.ds(0, NWA - 1)]
        pltpu.make_async_copy(others, others, recv_sem.at[chunk]).wait()
        rows = pl.ds(256 * chunk, 256)
        high[rows, :], low[rows, :] = split(landed[chunk].reshape(256, NX))

    def multiply(r, chunk):
        dot = functools.partial(lax.dot_general, dimension_numbers=NT, preferred_element_type=F32)
        for slot, (b, c) in enumerate(ROUNDS[r]):
            if c != chunk:
                continue
            hb, lb = high[pl.ds(256 * b, 256), :], low[pl.ds(256 * b, 256), :]
            hc, lc = high[pl.ds(256 * c, 256), :], low[pl.ds(256 * c, 256), :]
            block = dot(hb, hc) + (dot(hb, lc) + dot(lb, hc))
            gram[r, slot, 0] = block[:, :128]
            gram[r, slot, 1] = block[:, 128:]

    def send(src, dst, r, k, device):
        pltpu.make_async_remote_copy(
            src_ref=src, dst_ref=dst, send_sem=sem.at[0, r, k], recv_sem=sem.at[1, r, k],
            device_id=device, device_id_type=MESH,
        ).start()

    def wait(ref, r, k, way=1):
        pltpu.make_async_copy(ref, ref, sem.at[way, r, k]).wait()

    share = pl.ds(pl.multiple_of(16 * me_xy, 16), 16)

    def to_core(r):
        for slot in range(len(ROUNDS[r]), SLOTS):
            gram[r, slot] = jnp.zeros((2, 256, 128), F32)
        send(gram.at[r, :, other], from_core.at[r], r, 0, sibling)

    def to_xy(r):
        wait(from_core.at[r], r, 0)
        for slot in range(SLOTS):
            mine[r, :, slot] = (gram[r, slot, core] + from_core[r, slot]).reshape(NXY, 16, 128)

        @pl.loop(1, NXY)
        def _(step):
            q, device = xy_peer(step)
            send(mine.at[r, q], from_xy.at[r, me_xy], r, 1, device)

        from_xy[r, me_xy] = mine[r, me_xy]

    def to_z(r):
        wait(from_xy.at[r, pl.ds(0, NXY - 1)], r, 1)
        total = from_xy[r, 0]
        for q in range(1, NXY):
            total = total + from_xy[r, q]
        sums[r] = total.reshape(KZ, TILES, 128)

        @pl.loop(1, KZ)
        def _(step):
            q, device = z_peer(step)
            send(sums.at[r, q], from_z.at[r, z], r, 2, device)

        from_z[r, z] = sums[r, z]

    def back_z(r):
        wait(from_z.at[r, pl.ds(0, KZ - 1)], r, 2)
        total = from_z[r, 0]
        for q in range(1, KZ):
            total = total + from_z[r, q]
        final[r] = total
        gathered[r, z] = total

        @pl.loop(1, KZ)
        def _(step):
            q, device = z_peer(step)
            send(final.at[r], gathered.at[r, z], r, 3, device)

    def back_xy(r):
        wait(gathered.at[r, pl.ds(0, KZ - 1)], r, 3)
        part[r] = gathered[r].reshape(SLOTS, 16, 128)

        @pl.loop(1, NXY)
        def _(step):
            q, device = xy_peer(step)
            send(part.at[r], whole.at[r, :, core, share, :], r, 4, device)

        whole[r, :, core, share, :] = part[r]

    def back_core(r):
        wait(whole.at[r, :, 0, pl.ds(0, 240), :], r, 4)
        send(whole.at[r, :, core], whole.at[r, :, core], r, 5, sibling)

    def finish(r):
        wait(whole.at[r, :, other], r, 5)
        for slot, (b, c) in enumerate(ROUNDS[r]):
            block = jnp.concatenate([whole[r, slot, 0], whole[r, slot, 1]], axis=1) * (1.0 / 262144)
            rb, rc = pl.ds(256 * b, 256), pl.ds(256 * c, 256)
            gram_high[rb, rc], gram_low[rb, rc] = split(block)
            if b != c:
                gram_high[rc, rb], gram_low[rc, rb] = split(block.T)

    for chunk in range(CHUNKS):
        pack(chunk)
        send_chunk(chunk)
    take_chunk(0)
    multiply(0, 0)
    take_chunk(1)
    multiply(0, 1)
    to_core(0)
    to_xy(0)
    to_z(0)
    back_z(0)
    back_xy(0)
    take_chunk(2)
    multiply(1, 2)
    to_core(1)
    back_core(0)
    to_xy(1)
    finish(0)
    to_z(1)
    back_z(1)
    back_xy(1)
    take_chunk(3)
    multiply(2, 3)
    to_core(2)
    to_xy(2)
    back_core(1)
    finish(1)
    to_z(2)
    back_z(2)
    back_xy(2)
    back_core(2)
    finish(2)

    for c in range(CHUNKS):
        basis_ref[pl.ds(256 * c, 256), :] = start[:, c].reshape(256, RANK)

    @pl.loop(0, ITERS)
    def _(step):
        bh, bl = split(basis_ref[...])
        both = jnp.concatenate([bh, bl], axis=1)
        for c in range(CHUNKS):
            rows = pl.ds(256 * c, 256)
            wide = jnp.dot(gram_high[rows, :], both, preferred_element_type=F32)
            cross = jnp.dot(gram_low[rows, :], bh, preferred_element_type=F32)
            image_ref[rows, :] = wide[:, :RANK] + (wide[:, RANK:] + cross)
        image = image_ref[...]
        small = lax.dot_general(
            image, image, (((0,), (0,)), ((), ())), precision=lax.Precision.HIGHEST, preferred_element_type=F32
        )
        inverse_factor(small, lower_inv)
        basis_ref[...] = lax.dot_general(
            image, lower_inv[...], NT, precision=lax.Precision.HIGHEST, preferred_element_type=F32
        )

    basis = basis_ref[...]
    for c in range(CHUNKS):
        factor[:, c] = basis[256 * c : 256 * c + 256].reshape(NWA, 8, RANK)
    fh, fl = split(basis.T)
    both = jnp.concatenate([fh, fl], axis=0)
    for q in range(8):
        columns = pl.ds(128 * q, 128)
        wide = jnp.dot(both, high[:, columns], preferred_element_type=F32)
        cross = jnp.dot(fh, low[:, columns], preferred_element_type=F32)
        tile = wide[:RANK] + (wide[RANK:] + cross)
        for m in range(4):
            core_out[4 * q + m] = tile[:, 32 * m : 32 * m + 32]

    for chunk in range(CHUNKS):
        others = packed.at[chunk, pl.ds(0, NWA - 1)]
        pltpu.make_async_copy(others, others, send_sem.at[chunk]).wait()
    for r in range(len(ROUNDS)):
        wait(from_core.at[r], r, 0, 0)
        wait(mine.at[r, pl.ds(0, NXY - 1)], r, 1, 0)
        wait(sums.at[r, pl.ds(0, KZ - 1)], r, 2, 0)
        wait(gathered.at[r, pl.ds(0, KZ - 1)], r, 3, 0)
        wait(mine.at[r, pl.ds(0, NXY - 1)], r, 4, 0)
        wait(from_core.at[r], r, 5, 0)


def per_device(tensor, start):
    n = len(ROUNDS)
    factor, core = pl.pallas_call(
        kernel,
        out_shape=(
            jax.ShapeDtypeStruct((NWA, CHUNKS, 8, RANK), F32),
            jax.ShapeDtypeStruct((PLANES, RANK, 32), F32),
        ),
        in_specs=[pl.BlockSpec(memory_space=pl.ANY), pl.BlockSpec(memory_space=pltpu.VMEM)],
        out_specs=(pl.BlockSpec(memory_space=pltpu.VMEM),) * 2,
        scratch_shapes=[
            pltpu.VMEM((CHUNKS, PLANES, 8, NX), F32),
            pltpu.VMEM((CHUNKS, NWA, 8, NX), F32),
            pltpu.VMEM((CHUNKS, NWA, 8, NX), F32),
            pltpu.VMEM((NX, NX), BF16),
            pltpu.VMEM((NX, NX), BF16),
            pltpu.VMEM((n, SLOTS, 2, 256, 128), F32),
            pltpu.VMEM((n, SLOTS, 256, 128), F32),
            pltpu.VMEM((n, NXY, SLOTS, 16, 128), F32),
            pltpu.VMEM((n, NXY, SLOTS, 16, 128), F32),
            pltpu.VMEM((n, KZ, TILES, 128), F32),
            pltpu.VMEM((n, KZ, TILES, 128), F32),
            pltpu.VMEM((n, TILES, 128), F32),
            pltpu.VMEM((n, KZ, TILES, 128), F32),
            pltpu.VMEM((n, SLOTS, 16, 128), F32),
            pltpu.VMEM((n, SLOTS, 2, 256, 128), F32),
            pltpu.VMEM((NX, NX), BF16),
            pltpu.VMEM((NX, NX), BF16),
            pltpu.VMEM((NX, RANK), F32),
            pltpu.VMEM((NX, RANK), F32),
            pltpu.VMEM((RANK, RANK), F32),
            pltpu.SemaphoreType.DMA((CHUNKS,)),
            pltpu.SemaphoreType.DMA((CHUNKS,)),
            pltpu.SemaphoreType.DMA((CHUNKS,)),
            pltpu.SemaphoreType.DMA((2, n, 6)),
        ],
        compiler_params=pltpu.CompilerParams(
            collective_id=0, has_side_effects=True, vmem_limit_bytes=56 * 1024 * 1024
        ),
        name="factor_core",
    )(tensor.reshape(PLANES, 32, NX), start.reshape(NWA, CHUNKS, 8, RANK))
    return factor.reshape(NX, RANK), core.reshape(4, 8, RANK, 32)


def solution(mesh):
    placed = (P(None, "gz", "wa", None), P())
    return jax.shard_map(
        per_device,
        mesh=mesh,
        in_specs=placed,
        out_specs=(P(), P(None, "gz", None, "wa")),
        check_vma=False,
    )
```

```python
import functools

import jax
import jax.numpy as jnp
from jax import lax
from jax.experimental import pallas as pl
from jax.experimental.pallas import tpu as pltpu
from jax.sharding import PartitionSpec as P

MESH = pl.DeviceIdType.MESH
ITERS = 4
NX = 1024
RANK = 128
KX, KY, KZ = 4, 4, 8
NWA = KX * KZ
PLANES = 32
BATCH = 4
BATCHES = -(-(NWA - 1) // BATCH)
CHUNKS = 4
ROUNDS = [
    [(0, 0), (0, 1), (1, 1)],
    [(0, 2), (1, 2), (2, 2)],
    [(0, 3), (1, 3), (2, 3), (3, 3)],
]
SLOTS = 4
NXY = KX * KY
TILES = SLOTS * 2
F32, BF16 = jnp.float32, jnp.bfloat16
NT = (((1,), (1,)), ((), ()))


def split(values):
    high = values.astype(BF16)
    return high, (values - high.astype(F32)).astype(BF16)


def pack_tile(loaded, packed, chunk, quad):
    lane = lax.broadcasted_iota(jnp.int32, (8, 128), 1)
    low_half = lane < 64
    even_quarter = lax.rem(lane, 64) < 32
    for group in range(8):
        columns = pl.ds(128 * group, 128)
        v = [loaded[chunk, 4 * quad + m, :, columns] for m in range(4)]
        a = [None] * 4
        for m in range(2):
            a[m] = jnp.where(low_half, v[m], pltpu.roll(v[m + 2], 64, 1))
            a[m + 2] = jnp.where(low_half, pltpu.roll(v[m], 64, 1), v[m + 2])
        out = []
        for m in (0, 2):
            out.append(jnp.where(even_quarter, a[m], pltpu.roll(a[m + 1], 32, 1)))
            out.append(jnp.where(even_quarter, pltpu.roll(a[m], 96, 1), a[m + 1]))
        for m in range(4):
            packed[chunk, 4 * group + m, :, pl.ds(pl.multiple_of(128 * quad, 128), 128)] = out[m]


def inverse_factor(small, lower_inv):
    lane = lax.broadcasted_iota(jnp.int32, (8, RANK), 1)
    full = (8, RANK)
    count = RANK // 8
    tiles = [small[8 * t : 8 * t + 8, :] for t in range(count)]

    def columns(u, t):
        return [jnp.broadcast_to(tiles[u][:, 8 * t + s : 8 * t + s + 1], full) for s in range(8)]

    def spread(t):
        cols = columns(t, t)
        entry = {(i, s): jnp.broadcast_to(cols[s][i : i + 1, :], full) for s in range(8) for i in range(s, 8)}
        rows = []
        for s in range(8):
            row = jnp.broadcast_to(tiles[t][s : s + 1, :], full)
            inside = (lane >= 8 * t) & (lane < 8 * t + 8)
            rows.append(jnp.where(inside, jnp.where(lane == 8 * t + s, 1.0, 0.0), row))
        return entry, rows

    def update(u, t, lower, root, rows):
        cols = columns(u, t)
        inside = (lane >= 8 * t) & (lane < 8 * t + 8)
        tile = jnp.where(inside, 0.0, tiles[u])
        for k in range(8):
            cols[k] = cols[k] * root[k]
            for i in range(k + 1, 8):
                cols[i] = cols[i] - lower[i, k] * cols[k]
            tile = tile - cols[k] * rows[k]
        tiles[u] = tile

    entry, rows = spread(0)
    for t in range(count):
        root, lower = [], {}
        for k in range(8):
            root.append(lax.rsqrt(entry[k, k]))
            for i in range(k + 1, 8):
                lower[i, k] = entry[i, k] * root[k]
            for i in range(k + 1, 8):
                for j in range(k + 1, i + 1):
                    entry[i, j] = entry[i, j] - lower[i, k] * lower[j, k]
            rows[k] = rows[k] * root[k]
            for i in range(k + 1, 8):
                rows[i] = rows[i] - lower[i, k] * rows[k]
        done = rows
        if t + 1 < count:
            update(t + 1, t, lower, root, done)
            entry, rows = spread(t + 1)
        for u in range(t + 2, count):
            update(u, t, lower, root, done)
        for k in range(8):
            j = 8 * t + k
            lower_inv[j : j + 1, :] = jnp.where(lane <= j, done[k], 0.0)[0:1, :]


def kernel(
    tensor, start, factor, core_out,
    loaded, packed, landed, high, low,
    gram, from_core, mine, from_xy, sums, from_z, final, gathered, part, whole,
    gram_high, gram_low, basis_ref, image_ref, lower_inv,
    load_sem, send_sem, recv_sem, sem,
):
    me, gz = lax.axis_index("wa"), lax.axis_index("gz")
    x, z = me // KZ, lax.rem(me, KZ)
    y, core = gz // 2, lax.rem(gz, 2)
    me_xy = x * KY + y
    other = 1 - core
    sibling = {"gz": y * 2 + other}

    def peer(step):
        return lax.rem(me + step, NWA)

    def xy_peer(step):
        q = lax.rem(me_xy + step, NXY)
        return q, {"wa": (q // KY) * KZ + z, "gz": lax.rem(q, KY) * 2 + core}

    def z_peer(step):
        q = lax.rem(z + step, KZ)
        return q, {"wa": x * KZ + q}

    def load(chunk):
        return pltpu.make_async_copy(
            tensor.at[:, pl.ds(8 * chunk, 8), :], loaded.at[chunk], load_sem.at[chunk]
        )

    for chunk in range(CHUNKS):
        load(chunk).start()
    barrier = pltpu.get_barrier_semaphore()

    def greet(device):
        pl.semaphore_signal(barrier, inc=1, device_id=device, device_id_type=MESH)

    @pl.loop(1, NWA)
    def _(step):
        greet({"wa": peer(step)})

    @pl.loop(1, NXY)
    def _(step):
        greet(xy_peer(step)[1])

    greet(sibling)
    pl.semaphore_wait(barrier, NWA - 1 + NXY - 1 + 1)

    def pack(chunk):
        load(chunk).wait()

        @pl.loop(0, PLANES // 4)
        def _(quad):
            pack_tile(loaded, packed, chunk, quad)

    def batch(k):
        chunk, part = divmod(k, BATCHES)
        first = 1 + BATCH * part
        return chunk, part, first, min(first + BATCH, NWA)

    def send_batch(k):
        chunk, part, first, end = batch(k)

        @pl.loop(first, end)
        def _(step):
            half = lax.div(step + 1, 2)
            to = peer(jnp.where(lax.rem(step, 2) == 1, half, NWA - half))
            pltpu.make_async_remote_copy(
                src_ref=packed.at[chunk, to],
                dst_ref=landed.at[chunk, me],
                send_sem=send_sem.at[chunk, part],
                recv_sem=recv_sem.at[chunk],
                device_id={"wa": to},
                device_id_type=MESH,
            ).start()

        if part == 0:
            landed[chunk, me] = packed[chunk, me]

    def batch_left(k):
        chunk, part, first, end = batch(k)
        others = packed.at[chunk, pl.ds(0, end - first)]
        pltpu.make_async_copy(others, others, send_sem.at[chunk, part]).wait()

    def take_chunk(chunk):
        others = landed.at[chunk, pl.ds(0, NWA - 1)]
        pltpu.make_async_copy(others, others, recv_sem.at[chunk]).wait()
        rows = pl.ds(256 * chunk, 256)
        high[rows, :], low[rows, :] = split(landed[chunk].reshape(256, NX))

    def multiply(r, chunk):
        dot = functools.partial(lax.dot_general, dimension_numbers=NT, preferred_element_type=F32)
        for slot, (b, c) in enumerate(ROUNDS[r]):
            if c != chunk:
                continue
            hb, lb = high[pl.ds(256 * b, 256), :], low[pl.ds(256 * b, 256), :]
            hc, lc = high[pl.ds(256 * c, 256), :], low[pl.ds(256 * c, 256), :]
            block = dot(hb, hc) + (dot(hb, lc) + dot(lb, hc))
            gram[r, slot, 0] = block[:, :128]
            gram[r, slot, 1] = block[:, 128:]

    def send(src, dst, r, k, device):
        pltpu.make_async_remote_copy(
            src_ref=src, dst_ref=dst, send_sem=sem.at[0, r, k], recv_sem=sem.at[1, r, k],
            device_id=device, device_id_type=MESH,
        ).start()

    def wait(ref, r, k, way=1):
        pltpu.make_async_copy(ref, ref, sem.at[way, r, k]).wait()

    share = pl.ds(pl.multiple_of(16 * me_xy, 16), 16)

    def to_core(r):
        used = pl.ds(0, len(ROUNDS[r]))
        send(gram.at[r, used, other], from_core.at[r, used], r, 0, sibling)

    def to_xy(r):
        used = pl.ds(0, len(ROUNDS[r]))
        wait(from_core.at[r, used], r, 0)
        for slot in range(len(ROUNDS[r])):
            mine[r, :, slot] = (gram[r, slot, core] + from_core[r, slot]).reshape(NXY, 16, 128)

        @pl.loop(1, NXY)
        def _(step):
            q, device = xy_peer(step)
            send(mine.at[r, q, used], from_xy.at[r, me_xy, used], r, 1, device)

        from_xy[r, me_xy, used] = mine[r, me_xy, used]

    def to_z(r):
        n = len(ROUNDS[r])
        used = pl.ds(0, n)
        wait(from_xy.at[r, pl.ds(0, NXY - 1), used], r, 1)
        total = from_xy[r, 0, used]
        for q in range(1, NXY):
            total = total + from_xy[r, q, used]
        sums[r, pl.ds(0, 2 * n)] = total.reshape(2 * n, TILES, 128)
        if n < SLOTS:
            sums[r, pl.ds(2 * n, KZ - 2 * n)] = jnp.zeros((KZ - 2 * n, TILES, 128), F32)

        @pl.loop(1, KZ)
        def _(step):
            q, device = z_peer(step)
            send(sums.at[r, q], from_z.at[r, z], r, 2, device)

        from_z[r, z] = sums[r, z]

    def back_z(r):
        wait(from_z.at[r, pl.ds(0, KZ - 1)], r, 2)
        total = from_z[r, 0]
        for q in range(1, KZ):
            total = total + from_z[r, q]
        final[r] = total
        gathered[r, z] = total

        @pl.loop(1, KZ)
        def _(step):
            q, device = z_peer(step)
            send(final.at[r], gathered.at[r, z], r, 3, device)

    def back_xy(r):
        wait(gathered.at[r, pl.ds(0, KZ - 1)], r, 3)
        n = len(ROUNDS[r])
        used = pl.ds(0, n)
        part[r, used] = gathered[r, pl.ds(0, 2 * n)].reshape(n, 16, 128)

        @pl.loop(1, NXY)
        def _(step):
            q, device = xy_peer(step)
            send(part.at[r, used], whole.at[r, used, core, share, :], r, 4, device)

        whole[r, used, core, share, :] = part[r, used]

    def back_core(r):
        used = pl.ds(0, len(ROUNDS[r]))
        wait(whole.at[r, used, 0, pl.ds(0, 240), :], r, 4)
        send(whole.at[r, used, core], whole.at[r, used, core], r, 5, sibling)

    def finish(r):
        wait(from_core.at[r, pl.ds(0, len(ROUNDS[r]))], r, 5)
        for slot, (b, c) in enumerate(ROUNDS[r]):
            block = jnp.concatenate([whole[r, slot, 0], whole[r, slot, 1]], axis=1) * (1.0 / 262144)
            rb, rc = pl.ds(256 * b, 256), pl.ds(256 * c, 256)
            gram_high[rb, rc], gram_low[rb, rc] = split(block)
            if b != c:
                gram_high[rc, rb], gram_low[rc, rb] = split(block.T)

    pack(0)
    send_batch(0)
    pack(1)
    send_batch(1)
    batch_left(0)
    send_batch(2)
    batch_left(1)
    send_batch(3)
    batch_left(2)
    send_batch(4)
    batch_left(3)
    send_batch(5)
    batch_left(4)
    send_batch(6)
    batch_left(5)
    send_batch(7)
    batch_left(6)
    send_batch(8)
    pack(2)
    batch_left(7)
    send_batch(9)
    batch_left(8)
    send_batch(10)
    batch_left(9)
    send_batch(11)
    take_chunk(0)
    multiply(0, 0)
    batch_left(10)
    send_batch(12)
    batch_left(11)
    send_batch(13)
    batch_left(12)
    send_batch(14)
    batch_left(13)
    send_batch(15)
    batch_left(14)
    send_batch(16)
    pack(3)
    batch_left(15)
    send_batch(17)
    batch_left(16)
    send_batch(18)
    take_chunk(1)
    multiply(0, 1)
    to_core(0)
    batch_left(17)
    send_batch(19)
    batch_left(18)
    send_batch(20)
    to_xy(0)
    batch_left(19)
    send_batch(21)
    batch_left(20)
    send_batch(22)
    to_z(0)
    batch_left(21)
    send_batch(23)
    batch_left(22)
    send_batch(24)
    back_z(0)
    batch_left(23)
    send_batch(25)
    take_chunk(2)
    multiply(1, 2)
    to_core(1)
    batch_left(24)
    send_batch(26)
    back_xy(0)
    batch_left(25)
    send_batch(27)
    to_xy(1)
    batch_left(26)
    send_batch(28)
    back_core(0)
    batch_left(27)
    send_batch(29)
    batch_left(28)
    send_batch(30)
    batch_left(29)
    send_batch(31)
    finish(0)
    take_chunk(3)
    multiply(2, 3)
    to_z(1)
    to_core(2)
    to_xy(2)
    back_z(1)
    to_z(2)
    back_xy(1)
    back_z(2)
    back_core(1)
    finish(1)
    back_xy(2)
    back_core(2)
    finish(2)
    batch_left(30)
    batch_left(31)
    for c in range(CHUNKS):
        basis_ref[pl.ds(256 * c, 256), :] = start[:, c].reshape(256, RANK)

    @pl.loop(0, ITERS)
    def _(step):
        bh, bl = split(basis_ref[...])
        both = jnp.concatenate([bh, bl], axis=1)
        for c in range(CHUNKS):
            rows = pl.ds(256 * c, 256)
            wide = jnp.dot(gram_high[rows, :], both, preferred_element_type=F32)
            cross = jnp.dot(gram_low[rows, :], bh, preferred_element_type=F32)
            image_ref[rows, :] = wide[:, :RANK] + (wide[:, RANK:] + cross)
        image = image_ref[...]
        small = lax.dot_general(
            image, image, (((0,), (0,)), ((), ())), precision=lax.Precision.HIGHEST, preferred_element_type=F32
        )
        inverse_factor(small, lower_inv)
        basis_ref[...] = lax.dot_general(
            image, lower_inv[...], NT, precision=lax.Precision.HIGHEST, preferred_element_type=F32
        )

    basis = basis_ref[...]
    for c in range(CHUNKS):
        factor[:, c] = basis[256 * c : 256 * c + 256].reshape(NWA, 8, RANK)
    fh, fl = split(basis.T)
    both = jnp.concatenate([fh, fl], axis=0)
    for q in range(4):
        columns = pl.ds(256 * q, 256)
        wide = jnp.dot(both, high[:, columns], preferred_element_type=F32)
        cross = jnp.dot(fh, low[:, columns], preferred_element_type=F32)
        tile = (wide[:RANK] + (wide[RANK:] + cross)).T
        for m in range(8):
            core_out[8 * q + m] = tile[32 * m : 32 * m + 32]

    for r in range(len(ROUNDS)):
        used = pl.ds(0, len(ROUNDS[r]))
        wait(from_core.at[r, used], r, 0, 0)
        wait(mine.at[r, pl.ds(0, NXY - 1), used], r, 1, 0)
        wait(sums.at[r, pl.ds(0, KZ - 1)], r, 2, 0)
        wait(gathered.at[r, pl.ds(0, KZ - 1)], r, 3, 0)
        wait(mine.at[r, pl.ds(0, NXY - 1), used], r, 4, 0)
        wait(from_core.at[r, used], r, 5, 0)


def per_device(tensor, start):
    n = len(ROUNDS)
    factor, core = pl.pallas_call(
        kernel,
        out_shape=(
            jax.ShapeDtypeStruct((NWA, CHUNKS, 8, RANK), F32),
            jax.ShapeDtypeStruct((PLANES, 32, RANK), F32),
        ),
        in_specs=[pl.BlockSpec(memory_space=pl.ANY), pl.BlockSpec(memory_space=pltpu.VMEM)],
        out_specs=(pl.BlockSpec(memory_space=pltpu.VMEM),) * 2,
        scratch_shapes=[
            pltpu.VMEM((CHUNKS, PLANES, 8, NX), F32),
            pltpu.VMEM((CHUNKS, NWA, 8, NX), F32),
            pltpu.VMEM((CHUNKS, NWA, 8, NX), F32),
            pltpu.VMEM((NX, NX), BF16),
            pltpu.VMEM((NX, NX), BF16),
            pltpu.VMEM((n, SLOTS, 2, 256, 128), F32),
            pltpu.VMEM((n, SLOTS, 256, 128), F32),
            pltpu.VMEM((n, NXY, SLOTS, 16, 128), F32),
            pltpu.VMEM((n, NXY, SLOTS, 16, 128), F32),
            pltpu.VMEM((n, KZ, TILES, 128), F32),
            pltpu.VMEM((n, KZ, TILES, 128), F32),
            pltpu.VMEM((n, TILES, 128), F32),
            pltpu.VMEM((n, KZ, TILES, 128), F32),
            pltpu.VMEM((n, SLOTS, 16, 128), F32),
            pltpu.VMEM((n, SLOTS, 2, 256, 128), F32),
            pltpu.VMEM((NX, NX), BF16),
            pltpu.VMEM((NX, NX), BF16),
            pltpu.VMEM((NX, RANK), F32),
            pltpu.VMEM((NX, RANK), F32),
            pltpu.VMEM((RANK, RANK), F32),
            pltpu.SemaphoreType.DMA((CHUNKS,)),
            pltpu.SemaphoreType.DMA((CHUNKS, BATCHES)),
            pltpu.SemaphoreType.DMA((CHUNKS,)),
            pltpu.SemaphoreType.DMA((2, n, 6)),
        ],
        compiler_params=pltpu.CompilerParams(
            collective_id=0, has_side_effects=True, vmem_limit_bytes=56 * 1024 * 1024
        ),
        name="factor_core",
    )(tensor.reshape(PLANES, 32, NX), start.reshape(NWA, CHUNKS, 8, RANK))
    return factor.reshape(NX, RANK), jnp.swapaxes(core.reshape(4, 8, 32, RANK), 2, 3)


def solution(mesh):
    placed = (P(None, "gz", "wa", None), P())
    return jax.shard_map(
        per_device,
        mesh=mesh,
        in_specs=placed,
        out_specs=(P(), P(None, "gz", None, "wa")),
        check_vma=False,
    )
```

```python
import functools

import jax
import jax.numpy as jnp
from jax import lax
from jax.experimental import pallas as pl
from jax.experimental.pallas import tpu as pltpu
from jax.sharding import PartitionSpec as P

MESH = pl.DeviceIdType.MESH
ITERS = 4
NX = 1024
RANK = 128
KX, KY, KZ = 4, 4, 8
NWA = KX * KZ
PLANES = 32
BATCH = 4
BATCHES = -(-(NWA - 1) // BATCH)
CHUNKS = 4
ROUNDS = [
    [(0, 0), (0, 1), (1, 1)],
    [(0, 2), (1, 2), (2, 2)],
    [(0, 3), (1, 3), (2, 3), (3, 3)],
]
SLOTS = 4
NXY = KX * KY
TILES = SLOTS * 2
F32, BF16 = jnp.float32, jnp.bfloat16
NT = (((1,), (1,)), ((), ()))


def split(values):
    high = values.astype(BF16)
    return high, (values - high.astype(F32)).astype(BF16)


def pack_tile(loaded, packed, chunk, quad):
    lane = lax.broadcasted_iota(jnp.int32, (8, 128), 1)
    low_half = lane < 64
    even_quarter = lax.rem(lane, 64) < 32
    for group in range(8):
        columns = pl.ds(128 * group, 128)
        v = [loaded[chunk, 4 * quad + m, :, columns] for m in range(4)]
        a = [None] * 4
        for m in range(2):
            a[m] = jnp.where(low_half, v[m], pltpu.roll(v[m + 2], 64, 1))
            a[m + 2] = jnp.where(low_half, pltpu.roll(v[m], 64, 1), v[m + 2])
        out = []
        for m in (0, 2):
            out.append(jnp.where(even_quarter, a[m], pltpu.roll(a[m + 1], 32, 1)))
            out.append(jnp.where(even_quarter, pltpu.roll(a[m], 96, 1), a[m + 1]))
        for m in range(4):
            packed[chunk, 4 * group + m, :, pl.ds(pl.multiple_of(128 * quad, 128), 128)] = out[m]


def inverse_factor(small, lower_inv, stage):
    lane = lax.broadcasted_iota(jnp.int32, (8, RANK), 1)
    full = (8, RANK)
    sublane = lax.broadcasted_iota(jnp.int32, (8, RANK), 0)
    count = RANK // 8
    tiles = [small[8 * t : 8 * t + 8, :] for t in range(count)]

    def columns(u, t):
        return [jnp.broadcast_to(tiles[u][:, 8 * t + s : 8 * t + s + 1], full) for s in range(8)]

    def spread(t):
        cols = columns(t, t)
        slot = t % 2
        for s in range(8):
            stage[slot, s] = cols[s]
        stage[slot, 8] = tiles[t]
        entry = {(i, s): stage[slot, s, pl.ds(i, 8, stride=0), :] for s in range(8) for i in range(s, 8)}
        rows = []
        for s in range(8):
            row = stage[slot, 8, pl.ds(s, 8, stride=0), :]
            inside = (lane >= 8 * t) & (lane < 8 * t + 8)
            rows.append(jnp.where(inside, jnp.where(lane == 8 * t + s, 1.0, 0.0), row))
        return entry, rows

    def update(u, t, lower, root, rows):
        cols = columns(u, t)
        inside = (lane >= 8 * t) & (lane < 8 * t + 8)
        tile = jnp.where(inside, 0.0, tiles[u])
        for k in range(8):
            cols[k] = cols[k] * root[k]
            for i in range(k + 1, 8):
                cols[i] = cols[i] - lower[i, k] * cols[k]
            tile = tile - cols[k] * rows[k]
        tiles[u] = tile

    entry, rows = spread(0)
    for t in range(count):
        root, lower = [], {}
        for k in range(8):
            root.append(lax.rsqrt(entry[k, k]))
            for i in range(k + 1, 8):
                lower[i, k] = entry[i, k] * root[k]
            for i in range(k + 1, 8):
                for j in range(k + 1, i + 1):
                    entry[i, j] = entry[i, j] - lower[i, k] * lower[j, k]
            rows[k] = rows[k] * root[k]
            for i in range(k + 1, 8):
                rows[i] = rows[i] - lower[i, k] * rows[k]
        done = rows
        if t + 1 < count:
            update(t + 1, t, lower, root, done)
            entry, rows = spread(t + 1)
        for u in range(t + 2, min(t + 3, count)):
            update(u, t, lower, root, done)
        if t + 3 < count:
            block = done[0]
            for k in range(1, 8):
                block = jnp.where(sublane == k, done[k], block)
            hi, rest = block.astype(BF16), block - block.astype(BF16).astype(F32)
            mid, lo = split(rest)
            lhs = jnp.concatenate([hi, hi, hi, mid, mid, lo], axis=0)
            rhs = jnp.concatenate([hi, mid, lo, hi, mid, hi], axis=0)
            change = lax.dot_general(lhs, rhs, (((0,), (0,)), ((), ())), preferred_element_type=F32)
            inside = (lane >= 8 * t) & (lane < 8 * t + 8)
            for u in range(t + 3, count):
                tiles[u] = jnp.where(inside, 0.0, tiles[u]) - change[8 * u : 8 * u + 8]
        for k in range(8):
            j = 8 * t + k
            lower_inv[j : j + 1, :] = jnp.where(lane <= j, done[k], 0.0)[0:1, :]


def kernel(
    tensor, start, factor, core_out,
    loaded, packed, landed, high, low,
    gram, from_core, mine, from_xy, sums, from_z, final, gathered, part, whole,
    gram_high, gram_low, started, basis_ref, lower_inv, stage, factor_buf, core_buf,
    load_sem, send_sem, recv_sem, sem,
):
    me, gz = lax.axis_index("wa"), lax.axis_index("gz")
    x, z = me // KZ, lax.rem(me, KZ)
    y, core = gz // 2, lax.rem(gz, 2)
    me_xy = x * KY + y
    other = 1 - core
    sibling = {"gz": y * 2 + other}

    def peer(step):
        return lax.rem(me + step, NWA)

    def xy_peer(step):
        q = lax.rem(me_xy + step, NXY)
        return q, {"wa": (q // KY) * KZ + z, "gz": lax.rem(q, KY) * 2 + core}

    def z_peer(step):
        q = lax.rem(z + step, KZ)
        return q, {"wa": x * KZ + q}

    def load(chunk):
        return pltpu.make_async_copy(
            tensor.at[:, pl.ds(8 * chunk, 8), :], loaded.at[chunk], load_sem.at[chunk]
        )

    def load_start():
        return pltpu.make_async_copy(start, started, load_sem.at[CHUNKS])

    for chunk in range(CHUNKS):
        load(chunk).start()
    load_start().start()
    barrier = pltpu.get_barrier_semaphore()

    def greet(device):
        pl.semaphore_signal(barrier, inc=1, device_id=device, device_id_type=MESH)

    @pl.loop(1, NWA)
    def _(step):
        greet({"wa": peer(step)})

    @pl.loop(1, NXY)
    def _(step):
        greet(xy_peer(step)[1])

    greet(sibling)

    def pack(chunk):
        load(chunk).wait()

        @pl.loop(0, PLANES // 4)
        def _(quad):
            pack_tile(loaded, packed, chunk, quad)

    def batch(k):
        chunk, part = divmod(k, BATCHES)
        first = 1 + BATCH * part
        return chunk, part, first, min(first + BATCH, NWA)

    def send_batch(k):
        chunk, part, first, end = batch(k)

        @pl.loop(first, end)
        def _(step):
            half = lax.div(step + 1, 2)
            to = peer(jnp.where(lax.rem(step, 2) == 1, half, NWA - half))
            pltpu.make_async_remote_copy(
                src_ref=packed.at[chunk, to],
                dst_ref=landed.at[chunk, me],
                send_sem=send_sem.at[chunk, part],
                recv_sem=recv_sem.at[chunk],
                device_id={"wa": to},
                device_id_type=MESH,
            ).start()

        if part == 0:
            landed[chunk, me] = packed[chunk, me]

    def batch_left(k):
        chunk, part, first, end = batch(k)
        others = packed.at[chunk, pl.ds(0, end - first)]
        pltpu.make_async_copy(others, others, send_sem.at[chunk, part]).wait()

    def take_chunk(chunk):
        others = landed.at[chunk, pl.ds(0, NWA - 1)]
        pltpu.make_async_copy(others, others, recv_sem.at[chunk]).wait()
        rows = pl.ds(256 * chunk, 256)
        high[rows, :], low[rows, :] = split(landed[chunk].reshape(256, NX))

    def multiply(r, chunk):
        dot = functools.partial(lax.dot_general, dimension_numbers=NT, preferred_element_type=F32)
        for slot, (b, c) in enumerate(ROUNDS[r]):
            if c != chunk:
                continue
            hb, lb = high[pl.ds(256 * b, 256), :], low[pl.ds(256 * b, 256), :]
            hc, lc = high[pl.ds(256 * c, 256), :], low[pl.ds(256 * c, 256), :]
            block = dot(hb, hc) + (dot(hb, lc) + dot(lb, hc))
            gram[r, slot, 0] = block[:, :128]
            gram[r, slot, 1] = block[:, 128:]

    def send(src, dst, r, k, device):
        pltpu.make_async_remote_copy(
            src_ref=src, dst_ref=dst, send_sem=sem.at[0, r, k], recv_sem=sem.at[1, r, k],
            device_id=device, device_id_type=MESH,
        ).start()

    def wait(ref, r, k, way=1):
        pltpu.make_async_copy(ref, ref, sem.at[way, r, k]).wait()

    share = pl.ds(pl.multiple_of(16 * me_xy, 16), 16)

    def to_core(r):
        used = pl.ds(0, len(ROUNDS[r]))
        send(gram.at[r, used, other], from_core.at[r, used], r, 0, sibling)

    def to_xy(r):
        used = pl.ds(0, len(ROUNDS[r]))
        wait(from_core.at[r, used], r, 0)
        for slot in range(len(ROUNDS[r])):
            mine[r, :, slot] = (gram[r, slot, core] + from_core[r, slot]).reshape(NXY, 16, 128)

        @pl.loop(1, NXY)
        def _(step):
            q, device = xy_peer(step)
            send(mine.at[r, q, used], from_xy.at[r, me_xy, used], r, 1, device)

        from_xy[r, me_xy, used] = mine[r, me_xy, used]

    def to_z(r):
        n = len(ROUNDS[r])
        used = pl.ds(0, n)
        wait(from_xy.at[r, pl.ds(0, NXY - 1), used], r, 1)
        total = from_xy[r, 0, used]
        for q in range(1, NXY):
            total = total + from_xy[r, q, used]
        sums[r, pl.ds(0, 2 * n)] = total.reshape(2 * n, TILES, 128)
        if n < SLOTS:
            sums[r, pl.ds(2 * n, KZ - 2 * n)] = jnp.zeros((KZ - 2 * n, TILES, 128), F32)

        @pl.loop(1, KZ)
        def _(step):
            q, device = z_peer(step)
            send(sums.at[r, q], from_z.at[r, z], r, 2, device)

        from_z[r, z] = sums[r, z]

    def back_z(r):
        wait(from_z.at[r, pl.ds(0, KZ - 1)], r, 2)
        total = from_z[r, 0]
        for q in range(1, KZ):
            total = total + from_z[r, q]
        final[r] = total
        gathered[r, z] = total

        @pl.loop(1, KZ)
        def _(step):
            q, device = z_peer(step)
            send(final.at[r], gathered.at[r, z], r, 3, device)

    def back_xy(r):
        wait(gathered.at[r, pl.ds(0, KZ - 1)], r, 3)
        n = len(ROUNDS[r])
        used = pl.ds(0, n)
        part[r, used] = gathered[r, pl.ds(0, 2 * n)].reshape(n, 16, 128)

        @pl.loop(1, NXY)
        def _(step):
            q, device = xy_peer(step)
            send(part.at[r, used], whole.at[r, used, core, share, :], r, 4, device)

        whole[r, used, core, share, :] = part[r, used]

    def back_core(r):
        used = pl.ds(0, len(ROUNDS[r]))
        wait(whole.at[r, used, 0, pl.ds(0, 240), :], r, 4)
        send(whole.at[r, used, core], whole.at[r, used, core], r, 5, sibling)

    def finish(r):
        wait(from_core.at[r, pl.ds(0, len(ROUNDS[r]))], r, 5)
        for slot, (b, c) in enumerate(ROUNDS[r]):
            block = jnp.concatenate([whole[r, slot, 0], whole[r, slot, 1]], axis=1) * (1.0 / 262144)
            rb, rc = pl.ds(256 * b, 256), pl.ds(256 * c, 256)
            gram_high[rb, rc], gram_low[rb, rc] = split(block)
            if b != c:
                gram_high[rc, rb], gram_low[rc, rb] = split(block.T)

    pack(0)
    pl.semaphore_wait(barrier, NWA - 1 + NXY - 1 + 1)
    send_batch(0)
    pack(1)
    send_batch(1)
    batch_left(0)
    send_batch(2)
    batch_left(1)
    send_batch(3)
    batch_left(2)
    send_batch(4)
    batch_left(3)
    send_batch(5)
    batch_left(4)
    send_batch(6)
    batch_left(5)
    send_batch(7)
    batch_left(6)
    send_batch(8)
    pack(2)
    batch_left(7)
    send_batch(9)
    batch_left(8)
    send_batch(10)
    batch_left(9)
    send_batch(11)
    take_chunk(0)
    multiply(0, 0)
    batch_left(10)
    send_batch(12)
    batch_left(11)
    send_batch(13)
    batch_left(12)
    send_batch(14)
    batch_left(13)
    send_batch(15)
    batch_left(14)
    send_batch(16)
    pack(3)
    batch_left(15)
    send_batch(17)
    batch_left(16)
    send_batch(18)
    take_chunk(1)
    multiply(0, 1)
    to_core(0)
    batch_left(17)
    send_batch(19)
    batch_left(18)
    send_batch(20)
    to_xy(0)
    batch_left(19)
    send_batch(21)
    batch_left(20)
    send_batch(22)
    batch_left(21)
    send_batch(23)
    to_z(0)
    batch_left(22)
    send_batch(24)
    batch_left(23)
    send_batch(25)
    batch_left(24)
    send_batch(26)
    take_chunk(2)
    multiply(1, 2)
    to_core(1)
    back_z(0)
    batch_left(25)
    send_batch(27)
    batch_left(26)
    send_batch(28)
    to_xy(1)
    back_xy(0)
    batch_left(27)
    send_batch(29)
    batch_left(28)
    send_batch(30)
    batch_left(29)
    send_batch(31)
    back_core(0)
    take_chunk(3)
    multiply(2, 3)
    to_core(2)
    to_z(1)
    to_xy(2)
    finish(0)
    back_z(1)
    to_z(2)
    back_xy(1)
    back_z(2)
    back_core(1)
    finish(1)
    back_xy(2)
    back_core(2)
    finish(2)
    batch_left(30)
    batch_left(31)
    load_start().wait()
    for c in range(CHUNKS):
        basis_ref[:, pl.ds(256 * c, 256)] = started[:, c].reshape(256, RANK).T

    @pl.loop(0, ITERS)
    def _(step):
        bh, bl = split(basis_ref[...])
        both = jnp.concatenate([bh, bl], axis=0)
        wide = jnp.dot(both, gram_high[...], preferred_element_type=F32)
        cross = jnp.dot(bh, gram_low[...], preferred_element_type=F32)
        image = wide[:RANK] + (wide[RANK:] + cross)
        small = lax.dot_general(
            image, image, NT, precision=lax.Precision.HIGHEST, preferred_element_type=F32
        )
        inverse_factor(small, lower_inv, stage)
        basis_ref[...] = jnp.dot(
            lower_inv[...], image, precision=lax.Precision.HIGHEST, preferred_element_type=F32
        )

    basis = basis_ref[...]
    for c in range(CHUNKS):
        factor_buf[:, c] = basis[:, 256 * c : 256 * c + 256].T.reshape(NWA, 8, RANK)
    stored = [pltpu.make_async_copy(factor_buf, factor, load_sem.at[0])]
    stored[0].start()
    fh, fl = split(basis)
    both = jnp.concatenate([fh, fl], axis=0)
    for q in range(4):
        columns = pl.ds(256 * q, 256)
        wide = jnp.dot(both, high[:, columns], preferred_element_type=F32)
        cross = jnp.dot(fh, low[:, columns], preferred_element_type=F32)
        tile = (wide[:RANK] + (wide[RANK:] + cross)).T
        for m in range(8):
            core_buf[8 * q + m] = tile[32 * m : 32 * m + 32]
        planes = pl.ds(8 * q, 8)
        stored.append(pltpu.make_async_copy(core_buf.at[planes], core_out.at[planes], load_sem.at[1 + q]))
        stored[-1].start()

    for r in range(len(ROUNDS)):
        used = pl.ds(0, len(ROUNDS[r]))
        wait(from_core.at[r, used], r, 0, 0)
        wait(mine.at[r, pl.ds(0, NXY - 1), used], r, 1, 0)
        wait(sums.at[r, pl.ds(0, KZ - 1)], r, 2, 0)
        wait(gathered.at[r, pl.ds(0, KZ - 1)], r, 3, 0)
        wait(mine.at[r, pl.ds(0, NXY - 1), used], r, 4, 0)
        wait(from_core.at[r, used], r, 5, 0)
    for copy in stored:
        copy.wait()


def per_device(tensor, start):
    n = len(ROUNDS)
    factor, core = pl.pallas_call(
        kernel,
        out_shape=(
            jax.ShapeDtypeStruct((NWA, CHUNKS, 8, RANK), F32),
            jax.ShapeDtypeStruct((PLANES, 32, RANK), F32),
        ),
        in_specs=[pl.BlockSpec(memory_space=pl.ANY)] * 2,
        out_specs=(pl.BlockSpec(memory_space=pl.ANY),) * 2,
        scratch_shapes=[
            pltpu.VMEM((CHUNKS, PLANES, 8, NX), F32),
            pltpu.VMEM((CHUNKS, NWA, 8, NX), F32),
            pltpu.VMEM((CHUNKS, NWA, 8, NX), F32),
            pltpu.VMEM((NX, NX), BF16),
            pltpu.VMEM((NX, NX), BF16),
            pltpu.VMEM((n, SLOTS, 2, 256, 128), F32),
            pltpu.VMEM((n, SLOTS, 256, 128), F32),
            pltpu.VMEM((n, NXY, SLOTS, 16, 128), F32),
            pltpu.VMEM((n, NXY, SLOTS, 16, 128), F32),
            pltpu.VMEM((n, KZ, TILES, 128), F32),
            pltpu.VMEM((n, KZ, TILES, 128), F32),
            pltpu.VMEM((n, TILES, 128), F32),
            pltpu.VMEM((n, KZ, TILES, 128), F32),
            pltpu.VMEM((n, SLOTS, 16, 128), F32),
            pltpu.VMEM((n, SLOTS, 2, 256, 128), F32),
            pltpu.VMEM((NX, NX), BF16),
            pltpu.VMEM((NX, NX), BF16),
            pltpu.VMEM((NWA, CHUNKS, 8, RANK), F32),
            pltpu.VMEM((RANK, NX), F32),
            pltpu.VMEM((RANK, RANK), F32),
            pltpu.VMEM((2, 9, 8, RANK), F32),
            pltpu.VMEM((NWA, CHUNKS, 8, RANK), F32),
            pltpu.VMEM((PLANES, 32, RANK), F32),
            pltpu.SemaphoreType.DMA((CHUNKS + 1,)),
            pltpu.SemaphoreType.DMA((CHUNKS, BATCHES)),
            pltpu.SemaphoreType.DMA((CHUNKS,)),
            pltpu.SemaphoreType.DMA((2, n, 6)),
        ],
        compiler_params=pltpu.CompilerParams(
            collective_id=0, has_side_effects=True, vmem_limit_bytes=56 * 1024 * 1024
        ),
        name="factor_core",
    )(tensor.reshape(PLANES, 32, NX), start.reshape(NWA, CHUNKS, 8, RANK))
    return factor.reshape(NX, RANK), jnp.swapaxes(core.reshape(4, 8, 32, RANK), 2, 3)


def solution(mesh):
    placed = (P(None, "gz", "wa", None), P())
    return jax.shard_map(
        per_device,
        mesh=mesh,
        in_specs=placed,
        out_specs=(P(), P(None, "gz", None, "wa")),
        check_vma=False,
    )
```

```python
import functools

import jax
import jax.numpy as jnp
from jax import lax
from jax.experimental import pallas as pl
from jax.experimental.pallas import tpu as pltpu
from jax.sharding import PartitionSpec as P

MESH = pl.DeviceIdType.MESH
ITERS = 4
NX = 1024
RANK = 128
KX, KY, KZ = 4, 4, 8
NWA = KX * KZ
PLANES = 32
BATCH = 4
BATCHES = -(-(NWA - 1) // BATCH)
CHUNKS = 4
ROUNDS = [
    [(0, 0), (0, 1), (1, 1)],
    [(0, 2), (1, 2), (2, 2)],
    [(0, 3), (1, 3), (2, 3), (3, 3)],
]
SLOTS = 4
OFFSETS = [
    (2, 2), (2, 1), (1, 2), (2, 3), (3, 2), (2, 0), (0, 2), (1, 1),
    (3, 3), (1, 3), (3, 1), (1, 0), (0, 1), (3, 0), (0, 3),
]
NXY = KX * KY
TILES = SLOTS * 2
F32, BF16 = jnp.float32, jnp.bfloat16
NT = (((1,), (1,)), ((), ()))


def split(values):
    high = values.astype(BF16)
    return high, (values - high.astype(F32)).astype(BF16)


def pack_tile(loaded, packed, chunk, quad):
    lane = lax.broadcasted_iota(jnp.int32, (8, 128), 1)
    low_half = lane < 64
    even_quarter = lax.rem(lane, 64) < 32
    for group in range(8):
        columns = pl.ds(128 * group, 128)
        v = [loaded[chunk, 4 * quad + m, :, columns] for m in range(4)]
        a = [None] * 4
        for m in range(2):
            a[m] = jnp.where(low_half, v[m], pltpu.roll(v[m + 2], 64, 1))
            a[m + 2] = jnp.where(low_half, pltpu.roll(v[m], 64, 1), v[m + 2])
        out = []
        for m in (0, 2):
            out.append(jnp.where(even_quarter, a[m], pltpu.roll(a[m + 1], 32, 1)))
            out.append(jnp.where(even_quarter, pltpu.roll(a[m], 96, 1), a[m + 1]))
        for m in range(4):
            packed[chunk, 4 * group + m, :, pl.ds(pl.multiple_of(128 * quad, 128), 128)] = out[m]


def inverse_factor(small, lower_inv, stage):
    lane = lax.broadcasted_iota(jnp.int32, (8, RANK), 1)
    full = (8, RANK)
    sublane = lax.broadcasted_iota(jnp.int32, (8, RANK), 0)
    count = RANK // 8
    tiles = [small[8 * t : 8 * t + 8, :] for t in range(count)]

    def columns(u, t):
        return [jnp.broadcast_to(tiles[u][:, 8 * t + s : 8 * t + s + 1], full) for s in range(8)]

    def spread(t):
        cols = columns(t, t)
        slot = t % 2
        for s in range(8):
            stage[slot, s] = cols[s]
        stage[slot, 8] = tiles[t]
        entry = {(i, s): stage[slot, s, pl.ds(i, 8, stride=0), :] for s in range(8) for i in range(s, 8)}
        rows = []
        for s in range(8):
            row = stage[slot, 8, pl.ds(s, 8, stride=0), :]
            inside = (lane >= 8 * t) & (lane < 8 * t + 8)
            rows.append(jnp.where(inside, jnp.where(lane == 8 * t + s, 1.0, 0.0), row))
        return entry, rows

    def update(u, t, lower, root, rows):
        cols = columns(u, t)
        inside = (lane >= 8 * t) & (lane < 8 * t + 8)
        tile = jnp.where(inside, 0.0, tiles[u])
        for k in range(8):
            cols[k] = cols[k] * root[k]
            for i in range(k + 1, 8):
                cols[i] = cols[i] - lower[i, k] * cols[k]
            tile = tile - cols[k] * rows[k]
        tiles[u] = tile

    entry, rows = spread(0)
    for t in range(count):
        root, lower = [], {}
        for k in range(8):
            root.append(lax.rsqrt(entry[k, k]))
            for i in range(k + 1, 8):
                lower[i, k] = entry[i, k] * root[k]
            for i in range(k + 1, 8):
                for j in range(k + 1, i + 1):
                    entry[i, j] = entry[i, j] - lower[i, k] * lower[j, k]
            rows[k] = rows[k] * root[k]
            for i in range(k + 1, 8):
                rows[i] = rows[i] - lower[i, k] * rows[k]
        done = rows
        if t + 1 < count:
            update(t + 1, t, lower, root, done)
            entry, rows = spread(t + 1)
        for u in range(t + 2, min(t + 3, count)):
            update(u, t, lower, root, done)
        if t + 3 < count:
            block = done[0]
            for k in range(1, 8):
                block = jnp.where(sublane == k, done[k], block)
            hi, rest = block.astype(BF16), block - block.astype(BF16).astype(F32)
            mid, lo = split(rest)
            lhs = jnp.concatenate([hi, hi, hi, mid, mid, lo], axis=0)
            rhs = jnp.concatenate([hi, mid, lo, hi, mid, hi], axis=0)
            change = lax.dot_general(lhs, rhs, (((0,), (0,)), ((), ())), preferred_element_type=F32)
            inside = (lane >= 8 * t) & (lane < 8 * t + 8)
            for u in range(t + 3, count):
                tiles[u] = jnp.where(inside, 0.0, tiles[u]) - change[8 * u : 8 * u + 8]
        for k in range(8):
            j = 8 * t + k
            lower_inv[j : j + 1, :] = jnp.where(lane <= j, done[k], 0.0)[0:1, :]


def kernel(
    tensor, start, factor, core_out,
    loaded, packed, landed, high, low,
    gram, from_core, mine, from_xy, sums, from_z, final, gathered, part, whole,
    gram_high, gram_low, started, basis_ref, lower_inv, stage, factor_buf, core_buf,
    load_sem, send_sem, recv_sem, sem,
):
    me, gz = lax.axis_index("wa"), lax.axis_index("gz")
    x, z = me // KZ, lax.rem(me, KZ)
    y, core = gz // 2, lax.rem(gz, 2)
    me_xy = x * KY + y
    other = 1 - core
    sibling = {"gz": y * 2 + other}

    def peer(step):
        return lax.rem(me + step, NWA)

    def xy_peer(offset):
        to_x, to_y = lax.rem(x + offset[0], KX), lax.rem(y + offset[1], KY)
        return to_x * KY + to_y, {"wa": to_x * KZ + z, "gz": to_y * 2 + core}

    def z_peer(step):
        q = lax.rem(z + step, KZ)
        return q, {"wa": x * KZ + q}

    def load(chunk):
        return pltpu.make_async_copy(
            tensor.at[:, pl.ds(8 * chunk, 8), :], loaded.at[chunk], load_sem.at[chunk]
        )

    def load_start():
        return pltpu.make_async_copy(start, started, load_sem.at[CHUNKS])

    for chunk in range(CHUNKS):
        load(chunk).start()
    load_start().start()
    barrier = pltpu.get_barrier_semaphore()

    def greet(device):
        pl.semaphore_signal(barrier, inc=1, device_id=device, device_id_type=MESH)

    @pl.loop(1, NWA)
    def _(step):
        greet({"wa": peer(step)})

    for offset in OFFSETS:
        greet(xy_peer(offset)[1])

    greet(sibling)

    def pack(chunk):
        load(chunk).wait()

        @pl.loop(0, PLANES // 4)
        def _(quad):
            pack_tile(loaded, packed, chunk, quad)

    def batch(k):
        chunk, part = divmod(k, BATCHES)
        first = 1 + BATCH * part
        return chunk, part, first, min(first + BATCH, NWA)

    def send_batch(k):
        chunk, part, first, end = batch(k)

        @pl.loop(first, end)
        def _(step):
            rank = NWA - step
            half = lax.div(rank + 1, 2)
            to = peer(jnp.where(lax.rem(rank, 2) == 1, half, NWA - half))
            pltpu.make_async_remote_copy(
                src_ref=packed.at[chunk, to],
                dst_ref=landed.at[chunk, me],
                send_sem=send_sem.at[chunk, part],
                recv_sem=recv_sem.at[chunk],
                device_id={"wa": to},
                device_id_type=MESH,
            ).start()

        if part == 0:
            landed[chunk, me] = packed[chunk, me]

    def batch_left(k):
        chunk, part, first, end = batch(k)
        others = packed.at[chunk, pl.ds(0, end - first)]
        pltpu.make_async_copy(others, others, send_sem.at[chunk, part]).wait()

    def take_chunk(chunk):
        others = landed.at[chunk, pl.ds(0, NWA - 1)]
        pltpu.make_async_copy(others, others, recv_sem.at[chunk]).wait()
        rows = pl.ds(256 * chunk, 256)
        high[rows, :], low[rows, :] = split(landed[chunk].reshape(256, NX))

    def multiply(r, chunk):
        dot = functools.partial(lax.dot_general, dimension_numbers=NT, preferred_element_type=F32)
        for slot, (b, c) in enumerate(ROUNDS[r]):
            if c != chunk:
                continue
            hb, lb = high[pl.ds(256 * b, 256), :], low[pl.ds(256 * b, 256), :]
            hc, lc = high[pl.ds(256 * c, 256), :], low[pl.ds(256 * c, 256), :]
            block = dot(hb, hc) + (dot(hb, lc) + dot(lb, hc))
            gram[r, slot, 0] = block[:, :128]
            gram[r, slot, 1] = block[:, 128:]

    def send(src, dst, r, k, device):
        pltpu.make_async_remote_copy(
            src_ref=src, dst_ref=dst, send_sem=sem.at[0, r, k], recv_sem=sem.at[1, r, k],
            device_id=device, device_id_type=MESH,
        ).start()

    def wait(ref, r, k, way=1):
        pltpu.make_async_copy(ref, ref, sem.at[way, r, k]).wait()

    share = pl.ds(pl.multiple_of(16 * me_xy, 16), 16)

    def to_core(r):
        used = pl.ds(0, len(ROUNDS[r]))
        send(gram.at[r, used, other], from_core.at[r, used], r, 0, sibling)

    def to_xy(r):
        used = pl.ds(0, len(ROUNDS[r]))
        wait(from_core.at[r, used], r, 0)
        for slot in range(len(ROUNDS[r])):
            mine[r, :, slot] = (gram[r, slot, core] + from_core[r, slot]).reshape(NXY, 16, 128)

        for offset in OFFSETS:
            q, device = xy_peer(offset)
            send(mine.at[r, q, used], from_xy.at[r, me_xy, used], r, 1, device)

        from_xy[r, me_xy, used] = mine[r, me_xy, used]

    def to_z(r):
        n = len(ROUNDS[r])
        used = pl.ds(0, n)
        wait(from_xy.at[r, pl.ds(0, NXY - 1), used], r, 1)
        total = from_xy[r, 0, used]
        for q in range(1, NXY):
            total = total + from_xy[r, q, used]
        sums[r, pl.ds(0, 2 * n)] = total.reshape(2 * n, TILES, 128)
        if n < SLOTS:
            sums[r, pl.ds(2 * n, KZ - 2 * n)] = jnp.zeros((KZ - 2 * n, TILES, 128), F32)

        @pl.loop(1, KZ)
        def _(step):
            q, device = z_peer(step)
            send(sums.at[r, q], from_z.at[r, z], r, 2, device)

        from_z[r, z] = sums[r, z]

    def back_z(r):
        wait(from_z.at[r, pl.ds(0, KZ - 1)], r, 2)
        total = from_z[r, 0]
        for q in range(1, KZ):
            total = total + from_z[r, q]
        final[r] = total
        gathered[r, z] = total

        @pl.loop(1, KZ)
        def _(step):
            q, device = z_peer(step)
            send(final.at[r], gathered.at[r, z], r, 3, device)

    def back_xy(r):
        wait(gathered.at[r, pl.ds(0, KZ - 1)], r, 3)
        n = len(ROUNDS[r])
        used = pl.ds(0, n)
        part[r, used] = gathered[r, pl.ds(0, 2 * n)].reshape(n, 16, 128)

        for offset in OFFSETS:
            q, device = xy_peer(offset)
            send(part.at[r, used], whole.at[r, used, core, share, :], r, 4, device)

        whole[r, used, core, share, :] = part[r, used]

    def back_core(r):
        used = pl.ds(0, len(ROUNDS[r]))
        wait(whole.at[r, used, 0, pl.ds(0, 240), :], r, 4)
        send(whole.at[r, used, core], whole.at[r, used, core], r, 5, sibling)

    def finish(r):
        wait(from_core.at[r, pl.ds(0, len(ROUNDS[r]))], r, 5)
        for slot, (b, c) in enumerate(ROUNDS[r]):
            block = jnp.concatenate([whole[r, slot, 0], whole[r, slot, 1]], axis=1) * (1.0 / 262144)
            rb, rc = pl.ds(256 * b, 256), pl.ds(256 * c, 256)
            gram_high[rb, rc], gram_low[rb, rc] = split(block)
            if b != c:
                gram_high[rc, rb], gram_low[rc, rb] = split(block.T)

    pack(0)
    pl.semaphore_wait(barrier, NWA - 1 + NXY - 1 + 1)
    send_batch(0)
    pack(1)
    send_batch(1)
    batch_left(0)
    send_batch(2)
    batch_left(1)
    send_batch(3)
    batch_left(2)
    send_batch(4)
    batch_left(3)
    send_batch(5)
    batch_left(4)
    send_batch(6)
    batch_left(5)
    send_batch(7)
    batch_left(6)
    send_batch(8)
    pack(2)
    batch_left(7)
    send_batch(9)
    batch_left(8)
    send_batch(10)
    batch_left(9)
    send_batch(11)
    take_chunk(0)
    multiply(0, 0)
    batch_left(10)
    send_batch(12)
    batch_left(11)
    send_batch(13)
    batch_left(12)
    send_batch(14)
    batch_left(13)
    send_batch(15)
    batch_left(14)
    send_batch(16)
    pack(3)
    batch_left(15)
    send_batch(17)
    batch_left(16)
    send_batch(18)
    take_chunk(1)
    multiply(0, 1)
    to_core(0)
    batch_left(17)
    send_batch(19)
    batch_left(18)
    send_batch(20)
    to_xy(0)
    batch_left(19)
    send_batch(21)
    batch_left(20)
    send_batch(22)
    batch_left(21)
    send_batch(23)
    to_z(0)
    batch_left(22)
    send_batch(24)
    batch_left(23)
    send_batch(25)
    batch_left(24)
    send_batch(26)
    take_chunk(2)
    multiply(1, 2)
    to_core(1)
    back_z(0)
    batch_left(25)
    send_batch(27)
    batch_left(26)
    send_batch(28)
    to_xy(1)
    back_xy(0)
    batch_left(27)
    send_batch(29)
    batch_left(28)
    send_batch(30)
    batch_left(29)
    send_batch(31)
    back_core(0)
    take_chunk(3)
    multiply(2, 3)
    to_core(2)
    to_z(1)
    to_xy(2)
    finish(0)
    back_z(1)
    to_z(2)
    back_xy(1)
    back_z(2)
    back_core(1)
    finish(1)
    back_xy(2)
    back_core(2)
    finish(2)
    batch_left(30)
    batch_left(31)
    load_start().wait()
    for c in range(CHUNKS):
        basis_ref[:, pl.ds(256 * c, 256)] = started[:, c].reshape(256, RANK).T

    @pl.loop(0, ITERS)
    def _(step):
        bh, bl = split(basis_ref[...])
        both = jnp.concatenate([bh, bl], axis=0)
        wide = jnp.dot(both, gram_high[...], preferred_element_type=F32)
        cross = jnp.dot(bh, gram_low[...], preferred_element_type=F32)
        image = wide[:RANK] + (wide[RANK:] + cross)
        small = lax.dot_general(
            image, image, NT, precision=lax.Precision.HIGHEST, preferred_element_type=F32
        )
        inverse_factor(small, lower_inv, stage)
        ih, il = split(image)
        lh, ll = split(lower_inv[...])
        wide = jnp.dot(jnp.concatenate([lh, ll], axis=0), ih, preferred_element_type=F32)
        cross = jnp.dot(lh, il, preferred_element_type=F32)
        basis_ref[...] = wide[:RANK] + (wide[RANK:] + cross)

    basis = basis_ref[...]
    for c in range(CHUNKS):
        factor_buf[:, c] = basis[:, 256 * c : 256 * c + 256].T.reshape(NWA, 8, RANK)
    stored = [pltpu.make_async_copy(factor_buf, factor, load_sem.at[0])]
    stored[0].start()
    fh, fl = split(basis)
    both = jnp.concatenate([fh, fl], axis=0)
    for q in range(4):
        columns = pl.ds(256 * q, 256)
        wide = jnp.dot(both, high[:, columns], preferred_element_type=F32)
        cross = jnp.dot(fh, low[:, columns], preferred_element_type=F32)
        tile = (wide[:RANK] + (wide[RANK:] + cross)).T
        for m in range(8):
            core_buf[8 * q + m] = tile[32 * m : 32 * m + 32]
        planes = pl.ds(8 * q, 8)
        stored.append(pltpu.make_async_copy(core_buf.at[planes], core_out.at[planes], load_sem.at[1 + q]))
        stored[-1].start()

    for r in range(len(ROUNDS)):
        used = pl.ds(0, len(ROUNDS[r]))
        wait(from_core.at[r, used], r, 0, 0)
        wait(mine.at[r, pl.ds(0, NXY - 1), used], r, 1, 0)
        wait(sums.at[r, pl.ds(0, KZ - 1)], r, 2, 0)
        wait(gathered.at[r, pl.ds(0, KZ - 1)], r, 3, 0)
        wait(mine.at[r, pl.ds(0, NXY - 1), used], r, 4, 0)
        wait(from_core.at[r, used], r, 5, 0)
    for copy in stored:
        copy.wait()


def hand_over_kernel(factor, core, factor_out, core_out, buffers, sem):
    pairs = [(factor, factor_out), (core, core_out)]
    pieces = [(k, pl.ds(16 * part, 16)) for part in range(2) for k in range(2)]

    def fetch(n):
        k, rows = pieces[n]
        return pltpu.make_async_copy(pairs[k][0].at[rows], buffers.at[k, rows], sem.at[0, n])

    def store(n):
        k, rows = pieces[n]
        return pltpu.make_async_copy(buffers.at[k, rows], pairs[k][1].at[rows], sem.at[1, n])

    for n in range(len(pieces)):
        fetch(n).start()
    for n in range(len(pieces)):
        fetch(n).wait()
        store(n).start()
    for n in range(len(pieces)):
        store(n).wait()


def hand_over(factor, core):
    shape = jax.ShapeDtypeStruct((32, 32, RANK), F32)
    return pl.pallas_call(
        hand_over_kernel,
        out_shape=(shape, shape),
        in_specs=[pl.BlockSpec(memory_space=pl.ANY)] * 2,
        out_specs=(pl.BlockSpec(memory_space=pl.ANY),) * 2,
        scratch_shapes=[pltpu.VMEM((2, 32, 32, RANK), F32), pltpu.SemaphoreType.DMA((2, 4))],
        name="hand_over",
    )(factor, core)


def per_device(tensor, start):
    n = len(ROUNDS)
    factor, core = pl.pallas_call(
        kernel,
        out_shape=(
            jax.ShapeDtypeStruct((NWA, CHUNKS, 8, RANK), F32),
            jax.ShapeDtypeStruct((PLANES, 32, RANK), F32),
        ),
        in_specs=[pl.BlockSpec(memory_space=pl.ANY)] * 2,
        out_specs=(pl.BlockSpec(memory_space=pl.ANY),) * 2,
        scratch_shapes=[
            pltpu.VMEM((CHUNKS, PLANES, 8, NX), F32),
            pltpu.VMEM((CHUNKS, NWA, 8, NX), F32),
            pltpu.VMEM((CHUNKS, NWA, 8, NX), F32),
            pltpu.VMEM((NX, NX), BF16),
            pltpu.VMEM((NX, NX), BF16),
            pltpu.VMEM((n, SLOTS, 2, 256, 128), F32),
            pltpu.VMEM((n, SLOTS, 256, 128), F32),
            pltpu.VMEM((n, NXY, SLOTS, 16, 128), F32),
            pltpu.VMEM((n, NXY, SLOTS, 16, 128), F32),
            pltpu.VMEM((n, KZ, TILES, 128), F32),
            pltpu.VMEM((n, KZ, TILES, 128), F32),
            pltpu.VMEM((n, TILES, 128), F32),
            pltpu.VMEM((n, KZ, TILES, 128), F32),
            pltpu.VMEM((n, SLOTS, 16, 128), F32),
            pltpu.VMEM((n, SLOTS, 2, 256, 128), F32),
            pltpu.VMEM((NX, NX), BF16),
            pltpu.VMEM((NX, NX), BF16),
            pltpu.VMEM((NWA, CHUNKS, 8, RANK), F32),
            pltpu.VMEM((RANK, NX), F32),
            pltpu.VMEM((RANK, RANK), F32),
            pltpu.VMEM((2, 9, 8, RANK), F32),
            pltpu.VMEM((NWA, CHUNKS, 8, RANK), F32),
            pltpu.VMEM((PLANES, 32, RANK), F32),
            pltpu.SemaphoreType.DMA((CHUNKS + 1,)),
            pltpu.SemaphoreType.DMA((CHUNKS, BATCHES)),
            pltpu.SemaphoreType.DMA((CHUNKS,)),
            pltpu.SemaphoreType.DMA((2, n, 6)),
        ],
        compiler_params=pltpu.CompilerParams(
            collective_id=0, has_side_effects=True, vmem_limit_bytes=56 * 1024 * 1024
        ),
        name="factor_core",
    )(tensor.reshape(PLANES, 32, NX), start.reshape(NWA, CHUNKS, 8, RANK))
    factor, core = hand_over(factor.reshape(32, 32, RANK), core)
    return factor.reshape(NX, RANK), jnp.swapaxes(core.reshape(4, 8, 32, RANK), 2, 3)


def solution(mesh):
    placed = (P(None, "gz", "wa", None), P())
    return jax.shard_map(
        per_device,
        mesh=mesh,
        in_specs=placed,
        out_specs=(P(), P(None, "gz", None, "wa")),
        check_vma=False,
    )
```

```python
import functools

import jax
import jax.numpy as jnp
from jax import lax
from jax.experimental import pallas as pl
from jax.experimental.pallas import tpu as pltpu
from jax.sharding import PartitionSpec as P

MESH = pl.DeviceIdType.MESH
ITERS = 4
NX = 1024
RANK = 128
KX, KY, KZ = 4, 4, 8
NWA = KX * KZ
PLANES = 32
BATCH = 4
BATCHES = -(-(NWA - 1) // BATCH)
CHUNKS = 4
ROUNDS = [
    [(0, 0), (0, 1), (1, 1)],
    [(0, 2), (1, 2), (2, 2)],
    [(0, 3), (1, 3), (2, 3), (3, 3)],
]
SLOTS = 4
OFFSETS = [
    (2, 2), (2, 1), (1, 2), (2, 3), (3, 2), (2, 0), (0, 2), (1, 1),
    (3, 3), (1, 3), (3, 1), (1, 0), (0, 1), (3, 0), (0, 3),
]
NXY = KX * KY
TILES = SLOTS * 2
F32, BF16 = jnp.float32, jnp.bfloat16
NT = (((1,), (1,)), ((), ()))


def split(values):
    high = values.astype(BF16)
    return high, (values - high.astype(F32)).astype(BF16)


def pack_tile(loaded, packed, chunk, quad):
    lane = lax.broadcasted_iota(jnp.int32, (8, 128), 1)
    low_half = lane < 64
    even_quarter = lax.rem(lane, 64) < 32
    for group in range(8):
        columns = pl.ds(128 * group, 128)
        v = [loaded[chunk, 4 * quad + m, :, columns] for m in range(4)]
        a = [None] * 4
        for m in range(2):
            a[m] = jnp.where(low_half, v[m], pltpu.roll(v[m + 2], 64, 1))
            a[m + 2] = jnp.where(low_half, pltpu.roll(v[m], 64, 1), v[m + 2])
        out = []
        for m in (0, 2):
            out.append(jnp.where(even_quarter, a[m], pltpu.roll(a[m + 1], 32, 1)))
            out.append(jnp.where(even_quarter, pltpu.roll(a[m], 96, 1), a[m + 1]))
        for m in range(4):
            packed[chunk, 4 * group + m, :, pl.ds(pl.multiple_of(128 * quad, 128), 128)] = out[m]


def inverse_factor(small, lower_inv, stage):
    lane = lax.broadcasted_iota(jnp.int32, (8, RANK), 1)
    full = (8, RANK)
    sublane = lax.broadcasted_iota(jnp.int32, (8, RANK), 0)
    count = RANK // 8
    tiles = [small[8 * t : 8 * t + 8, :] for t in range(count)]

    def columns(u, t):
        return [jnp.broadcast_to(tiles[u][:, 8 * t + s : 8 * t + s + 1], full) for s in range(8)]

    def spread(t):
        cols = columns(t, t)
        slot = t % 2
        for s in range(8):
            stage[slot, s] = cols[s]
        stage[slot, 8] = tiles[t]
        entry = {(i, s): stage[slot, s, pl.ds(i, 8, stride=0), :] for s in range(8) for i in range(s, 8)}
        rows = []
        for s in range(8):
            row = stage[slot, 8, pl.ds(s, 8, stride=0), :]
            inside = (lane >= 8 * t) & (lane < 8 * t + 8)
            rows.append(jnp.where(inside, jnp.where(lane == 8 * t + s, 1.0, 0.0), row))
        return entry, rows

    def update(u, t, lower, root, rows):
        cols = columns(u, t)
        inside = (lane >= 8 * t) & (lane < 8 * t + 8)
        tile = jnp.where(inside, 0.0, tiles[u])
        for k in range(8):
            cols[k] = cols[k] * root[k]
            for i in range(k + 1, 8):
                cols[i] = cols[i] - lower[i, k] * cols[k]
            tile = tile - cols[k] * rows[k]
        tiles[u] = tile

    entry, rows = spread(0)
    for t in range(count):
        root, lower = [], {}
        for k in range(8):
            root.append(lax.rsqrt(entry[k, k]))
            for i in range(k + 1, 8):
                lower[i, k] = entry[i, k] * root[k]
            for i in range(k + 1, 8):
                for j in range(k + 1, i + 1):
                    entry[i, j] = entry[i, j] - lower[i, k] * lower[j, k]
            rows[k] = rows[k] * root[k]
            for i in range(k + 1, 8):
                rows[i] = rows[i] - lower[i, k] * rows[k]
        done = rows
        if t + 1 < count:
            update(t + 1, t, lower, root, done)
            entry, rows = spread(t + 1)
        for u in range(t + 2, min(t + 3, count)):
            update(u, t, lower, root, done)
        if t + 3 < count:
            block = done[0]
            for k in range(1, 8):
                block = jnp.where(sublane == k, done[k], block)
            hi, rest = block.astype(BF16), block - block.astype(BF16).astype(F32)
            mid, lo = split(rest)
            lhs = jnp.concatenate([hi, hi, hi, mid, mid, lo], axis=0)
            rhs = jnp.concatenate([hi, mid, lo, hi, mid, hi], axis=0)
            change = lax.dot_general(lhs, rhs, (((0,), (0,)), ((), ())), preferred_element_type=F32)
            inside = (lane >= 8 * t) & (lane < 8 * t + 8)
            for u in range(t + 3, count):
                tiles[u] = jnp.where(inside, 0.0, tiles[u]) - change[8 * u : 8 * u + 8]
        for k in range(8):
            j = 8 * t + k
            lower_inv[j : j + 1, :] = jnp.where(lane <= j, done[k], 0.0)[0:1, :]


def kernel(
    tensor, start, factor, core_out,
    loaded, packed, landed, high, low,
    gram, from_core, mine, from_xy, sums, from_z, final, gathered, part, whole,
    gram_high, gram_low, started, basis_ref, lower_inv, stage, factor_buf, core_buf,
    load_sem, send_sem, recv_sem, sem,
):
    me, gz = lax.axis_index("wa"), lax.axis_index("gz")
    x, z = me // KZ, lax.rem(me, KZ)
    y, core = gz // 2, lax.rem(gz, 2)
    me_xy = x * KY + y
    other = 1 - core
    sibling = {"gz": y * 2 + other}

    def peer(step):
        return lax.rem(me + step, NWA)

    def xy_peer(offset):
        to_x, to_y = lax.rem(x + offset[0], KX), lax.rem(y + offset[1], KY)
        return to_x * KY + to_y, {"wa": to_x * KZ + z, "gz": to_y * 2 + core}

    def z_peer(step):
        q = lax.rem(z + step, KZ)
        return q, {"wa": x * KZ + q}

    def load(chunk):
        return pltpu.make_async_copy(
            tensor.at[:, pl.ds(8 * chunk, 8), :], loaded.at[chunk], load_sem.at[chunk]
        )

    def load_start():
        return pltpu.make_async_copy(start, started, load_sem.at[CHUNKS])

    for chunk in range(CHUNKS):
        load(chunk).start()
    load_start().start()
    barrier = pltpu.get_barrier_semaphore()

    def greet(device):
        pl.semaphore_signal(barrier, inc=1, device_id=device, device_id_type=MESH)

    @pl.loop(1, NWA)
    def _(step):
        greet({"wa": peer(step)})

    for offset in OFFSETS:
        greet(xy_peer(offset)[1])

    greet(sibling)

    def pack(chunk):
        load(chunk).wait()

        @pl.loop(0, PLANES // 4)
        def _(quad):
            pack_tile(loaded, packed, chunk, quad)

    def batch(k):
        chunk, part = divmod(k, BATCHES)
        first = 1 + BATCH * part
        return chunk, part, first, min(first + BATCH, NWA)

    def send_batch(k):
        chunk, part, first, end = batch(k)

        @pl.loop(first, end)
        def _(step):
            rank = NWA - step
            half = lax.div(rank + 1, 2)
            to = peer(jnp.where(lax.rem(rank, 2) == 1, half, NWA - half))
            pltpu.make_async_remote_copy(
                src_ref=packed.at[chunk, to],
                dst_ref=landed.at[chunk, me],
                send_sem=send_sem.at[chunk, part],
                recv_sem=recv_sem.at[chunk],
                device_id={"wa": to},
                device_id_type=MESH,
            ).start()

        if part == 0:
            landed[chunk, me] = packed[chunk, me]

    def batch_left(k):
        chunk, part, first, end = batch(k)
        others = packed.at[chunk, pl.ds(0, end - first)]
        pltpu.make_async_copy(others, others, send_sem.at[chunk, part]).wait()

    def take_chunk(chunk):
        others = landed.at[chunk, pl.ds(0, NWA - 1)]
        pltpu.make_async_copy(others, others, recv_sem.at[chunk]).wait()
        rows = pl.ds(256 * chunk, 256)
        high[rows, :], low[rows, :] = split(landed[chunk].reshape(256, NX))

    def multiply(r, chunk):
        dot = functools.partial(lax.dot_general, dimension_numbers=NT, preferred_element_type=F32)
        for slot, (b, c) in enumerate(ROUNDS[r]):
            if c != chunk:
                continue
            hb, lb = high[pl.ds(256 * b, 256), :], low[pl.ds(256 * b, 256), :]
            hc, lc = high[pl.ds(256 * c, 256), :], low[pl.ds(256 * c, 256), :]
            block = dot(hb, hc) + (dot(hb, lc) + dot(lb, hc))
            gram[r, slot, 0] = block[:, :128]
            gram[r, slot, 1] = block[:, 128:]

    def send(src, dst, r, k, device):
        pltpu.make_async_remote_copy(
            src_ref=src, dst_ref=dst, send_sem=sem.at[0, r, k], recv_sem=sem.at[1, r, k],
            device_id=device, device_id_type=MESH,
        ).start()

    def wait(ref, r, k, way=1):
        pltpu.make_async_copy(ref, ref, sem.at[way, r, k]).wait()

    share = pl.ds(pl.multiple_of(16 * me_xy, 16), 16)

    def to_core(r):
        used = pl.ds(0, len(ROUNDS[r]))
        send(gram.at[r, used, other], from_core.at[r, used], r, 0, sibling)

    def to_xy(r):
        used = pl.ds(0, len(ROUNDS[r]))
        wait(from_core.at[r, used], r, 0)
        for slot in range(len(ROUNDS[r])):
            mine[r, :, slot] = (gram[r, slot, core] + from_core[r, slot]).reshape(NXY, 16, 128)

        for offset in OFFSETS:
            q, device = xy_peer(offset)
            send(mine.at[r, q, used], from_xy.at[r, me_xy, used], r, 1, device)

        from_xy[r, me_xy, used] = mine[r, me_xy, used]

    def to_z(r):
        n = len(ROUNDS[r])
        used = pl.ds(0, n)
        wait(from_xy.at[r, pl.ds(0, NXY - 1), used], r, 1)
        total = from_xy[r, 0, used]
        for q in range(1, NXY):
            total = total + from_xy[r, q, used]
        sums[r, pl.ds(0, 2 * n)] = total.reshape(2 * n, TILES, 128)
        if n < SLOTS:
            sums[r, pl.ds(2 * n, KZ - 2 * n)] = jnp.zeros((KZ - 2 * n, TILES, 128), F32)

        @pl.loop(1, KZ)
        def _(step):
            q, device = z_peer(step)
            send(sums.at[r, q], from_z.at[r, z], r, 2, device)

        from_z[r, z] = sums[r, z]

    def back_z(r):
        wait(from_z.at[r, pl.ds(0, KZ - 1)], r, 2)
        total = from_z[r, 0]
        for q in range(1, KZ):
            total = total + from_z[r, q]
        final[r] = total
        gathered[r, z] = total

        @pl.loop(1, KZ)
        def _(step):
            q, device = z_peer(step)
            send(final.at[r], gathered.at[r, z], r, 3, device)

    def back_xy(r):
        wait(gathered.at[r, pl.ds(0, KZ - 1)], r, 3)
        n = len(ROUNDS[r])
        used = pl.ds(0, n)
        part[r, used] = gathered[r, pl.ds(0, 2 * n)].reshape(n, 16, 128)

        for offset in OFFSETS:
            q, device = xy_peer(offset)
            send(part.at[r, used], whole.at[r, used, core, share, :], r, 4, device)

        whole[r, used, core, share, :] = part[r, used]

    def back_core(r):
        used = pl.ds(0, len(ROUNDS[r]))
        wait(whole.at[r, used, 0, pl.ds(0, 240), :], r, 4)
        send(whole.at[r, used, core], whole.at[r, used, core], r, 5, sibling)

    def finish(r):
        wait(from_core.at[r, pl.ds(0, len(ROUNDS[r]))], r, 5)
        for slot, (b, c) in enumerate(ROUNDS[r]):
            block = jnp.concatenate([whole[r, slot, 0], whole[r, slot, 1]], axis=1) * (1.0 / 262144)
            rb, rc = pl.ds(256 * b, 256), pl.ds(256 * c, 256)
            gram_high[rb, rc], gram_low[rb, rc] = split(block)
            if b != c:
                gram_high[rc, rb], gram_low[rc, rb] = split(block.T)

    pack(0)
    pl.semaphore_wait(barrier, NWA - 1 + NXY - 1 + 1)
    send_batch(0)
    pack(1)
    send_batch(1)
    batch_left(0)
    send_batch(2)
    batch_left(1)
    send_batch(3)
    batch_left(2)
    send_batch(4)
    batch_left(3)
    send_batch(5)
    batch_left(4)
    send_batch(6)
    batch_left(5)
    send_batch(7)
    batch_left(6)
    send_batch(8)
    pack(2)
    batch_left(7)
    send_batch(9)
    batch_left(8)
    send_batch(10)
    batch_left(9)
    send_batch(11)
    take_chunk(0)
    multiply(0, 0)
    batch_left(10)
    send_batch(12)
    batch_left(11)
    send_batch(13)
    batch_left(12)
    send_batch(14)
    batch_left(13)
    send_batch(15)
    batch_left(14)
    send_batch(16)
    pack(3)
    batch_left(15)
    send_batch(17)
    batch_left(16)
    send_batch(18)
    take_chunk(1)
    multiply(0, 1)
    to_core(0)
    batch_left(17)
    send_batch(19)
    batch_left(18)
    send_batch(20)
    to_xy(0)
    batch_left(19)
    send_batch(21)
    batch_left(20)
    send_batch(22)
    batch_left(21)
    send_batch(23)
    to_z(0)
    batch_left(22)
    send_batch(24)
    batch_left(23)
    send_batch(25)
    batch_left(24)
    send_batch(26)
    take_chunk(2)
    multiply(1, 2)
    to_core(1)
    back_z(0)
    batch_left(25)
    send_batch(27)
    batch_left(26)
    send_batch(28)
    to_xy(1)
    back_xy(0)
    batch_left(27)
    send_batch(29)
    batch_left(28)
    send_batch(30)
    batch_left(29)
    send_batch(31)
    back_core(0)
    to_z(1)
    take_chunk(3)
    multiply(2, 3)
    to_core(2)
    to_xy(2)
    finish(0)
    back_z(1)
    to_z(2)
    back_xy(1)
    back_z(2)
    back_core(1)
    finish(1)
    back_xy(2)
    back_core(2)
    finish(2)
    batch_left(30)
    batch_left(31)
    load_start().wait()
    for c in range(CHUNKS):
        basis_ref[:, pl.ds(256 * c, 256)] = started[:, c].reshape(256, RANK).T

    @pl.loop(0, ITERS)
    def _(step):
        bh, bl = split(basis_ref[...])
        both = jnp.concatenate([bh, bl], axis=0)
        wide = jnp.dot(both, gram_high[...], preferred_element_type=F32)
        cross = jnp.dot(bh, gram_low[...], preferred_element_type=F32)
        image = wide[:RANK] + (wide[RANK:] + cross)
        small = lax.dot_general(
            image, image, NT, precision=lax.Precision.HIGHEST, preferred_element_type=F32
        )
        inverse_factor(small, lower_inv, stage)
        ih, il = split(image)
        lh, ll = split(lower_inv[...])
        wide = jnp.dot(jnp.concatenate([lh, ll], axis=0), ih, preferred_element_type=F32)
        cross = jnp.dot(lh, il, preferred_element_type=F32)
        basis_ref[...] = wide[:RANK] + (wide[RANK:] + cross)

    basis = basis_ref[...]
    for c in range(CHUNKS):
        factor_buf[:, c] = basis[:, 256 * c : 256 * c + 256].T.reshape(NWA, 8, RANK)
    stored = [pltpu.make_async_copy(factor_buf, factor, load_sem.at[0])]
    stored[0].start()
    fh, fl = split(basis)
    both = jnp.concatenate([fh, fl], axis=0)
    for q in range(4):
        columns = pl.ds(256 * q, 256)
        wide = jnp.dot(both, high[:, columns], preferred_element_type=F32)
        cross = jnp.dot(fh, low[:, columns], preferred_element_type=F32)
        tile = (wide[:RANK] + (wide[RANK:] + cross)).T
        for m in range(8):
            core_buf[8 * q + m] = tile[32 * m : 32 * m + 32]
        planes = pl.ds(8 * q, 8)
        stored.append(pltpu.make_async_copy(core_buf.at[planes], core_out.at[planes], load_sem.at[1 + q]))
        stored[-1].start()

    for r in range(len(ROUNDS)):
        used = pl.ds(0, len(ROUNDS[r]))
        wait(from_core.at[r, used], r, 0, 0)
        wait(mine.at[r, pl.ds(0, NXY - 1), used], r, 1, 0)
        wait(sums.at[r, pl.ds(0, KZ - 1)], r, 2, 0)
        wait(gathered.at[r, pl.ds(0, KZ - 1)], r, 3, 0)
        wait(mine.at[r, pl.ds(0, NXY - 1), used], r, 4, 0)
        wait(from_core.at[r, used], r, 5, 0)
    for copy in stored:
        copy.wait()


def hand_over_kernel(factor, core, factor_out, core_out, buffers, sem):
    pairs = [(factor, factor_out), (core, core_out)]
    pieces = [(k, pl.ds(16 * part, 16)) for part in range(2) for k in range(2)]

    def fetch(n):
        k, rows = pieces[n]
        return pltpu.make_async_copy(pairs[k][0].at[rows], buffers.at[k, rows], sem.at[0, n])

    def store(n):
        k, rows = pieces[n]
        return pltpu.make_async_copy(buffers.at[k, rows], pairs[k][1].at[rows], sem.at[1, n])

    for n in range(len(pieces)):
        fetch(n).start()
    for n in range(len(pieces)):
        fetch(n).wait()
        store(n).start()
    for n in range(len(pieces)):
        store(n).wait()


def hand_over(factor, core):
    shape = jax.ShapeDtypeStruct((32, 32, RANK), F32)
    return pl.pallas_call(
        hand_over_kernel,
        out_shape=(shape, shape),
        in_specs=[pl.BlockSpec(memory_space=pl.ANY)] * 2,
        out_specs=(pl.BlockSpec(memory_space=pl.ANY),) * 2,
        scratch_shapes=[pltpu.VMEM((2, 32, 32, RANK), F32), pltpu.SemaphoreType.DMA((2, 4))],
        name="hand_over",
    )(factor, core)


def per_device(tensor, start):
    n = len(ROUNDS)
    factor, core = pl.pallas_call(
        kernel,
        out_shape=(
            jax.ShapeDtypeStruct((NWA, CHUNKS, 8, RANK), F32),
            jax.ShapeDtypeStruct((PLANES, 32, RANK), F32),
        ),
        in_specs=[pl.BlockSpec(memory_space=pl.ANY)] * 2,
        out_specs=(pl.BlockSpec(memory_space=pl.ANY),) * 2,
        scratch_shapes=[
            pltpu.VMEM((CHUNKS, PLANES, 8, NX), F32),
            pltpu.VMEM((CHUNKS, NWA, 8, NX), F32),
            pltpu.VMEM((CHUNKS, NWA, 8, NX), F32),
            pltpu.VMEM((NX, NX), BF16),
            pltpu.VMEM((NX, NX), BF16),
            pltpu.VMEM((n, SLOTS, 2, 256, 128), F32),
            pltpu.VMEM((n, SLOTS, 256, 128), F32),
            pltpu.VMEM((n, NXY, SLOTS, 16, 128), F32),
            pltpu.VMEM((n, NXY, SLOTS, 16, 128), F32),
            pltpu.VMEM((n, KZ, TILES, 128), F32),
            pltpu.VMEM((n, KZ, TILES, 128), F32),
            pltpu.VMEM((n, TILES, 128), F32),
            pltpu.VMEM((n, KZ, TILES, 128), F32),
            pltpu.VMEM((n, SLOTS, 16, 128), F32),
            pltpu.VMEM((n, SLOTS, 2, 256, 128), F32),
            pltpu.VMEM((NX, NX), BF16),
            pltpu.VMEM((NX, NX), BF16),
            pltpu.VMEM((NWA, CHUNKS, 8, RANK), F32),
            pltpu.VMEM((RANK, NX), F32),
            pltpu.VMEM((RANK, RANK), F32),
            pltpu.VMEM((2, 9, 8, RANK), F32),
            pltpu.VMEM((NWA, CHUNKS, 8, RANK), F32),
            pltpu.VMEM((PLANES, 32, RANK), F32),
            pltpu.SemaphoreType.DMA((CHUNKS + 1,)),
            pltpu.SemaphoreType.DMA((CHUNKS, BATCHES)),
            pltpu.SemaphoreType.DMA((CHUNKS,)),
            pltpu.SemaphoreType.DMA((2, n, 6)),
        ],
        compiler_params=pltpu.CompilerParams(
            collective_id=0, has_side_effects=True, vmem_limit_bytes=56 * 1024 * 1024
        ),
        name="factor_core",
    )(tensor.reshape(PLANES, 32, NX), start.reshape(NWA, CHUNKS, 8, RANK))
    factor, core = hand_over(factor.reshape(32, 32, RANK), core)
    return factor.reshape(NX, RANK), jnp.swapaxes(core.reshape(4, 8, 32, RANK), 2, 3)


def solution(mesh):
    placed = (P(None, "gz", "wa", None), P())
    return jax.shard_map(
        per_device,
        mesh=mesh,
        in_specs=placed,
        out_specs=(P(), P(None, "gz", None, "wa")),
        check_vma=False,
    )
```
